32 devices in a mesh: groups: 2 (over y), patch: 4 (over z), ccd: 4 (over x, core).
Axes of the slice: x: 2, y: 2, z: 4, core: 2. Of those that a mesh axis runs over, the one named last changes fastest.
Arguments:
- science: bfloat16 [512, 48, 128], P(('groups', 'patch', 'ccd')), parts along dimension 0
- strip_patch: int32 [512], P(('groups', 'patch', 'ccd')), parts along dimension 0, may hold values from 0 to 3, as said below
- strip_tile: int32 [512], P(('groups', 'patch', 'ccd')), parts along dimension 0, may hold values from 0 to 15
- strip_row: int32 [512], P(('groups', 'patch', 'ccd')), parts along dimension 0, may hold values from 0 to 3952
- row_count: int32 [512], P(('groups', 'patch', 'ccd')), parts along dimension 0, may hold values from 24 to 48
- template: bfloat16 [512, 80, 128], P(('groups', 'patch', 'ccd')), parts along dimension 0
- basis_rows: bfloat16 [14, 21], replicated, may hold values from -1.25 to 1.25
- basis_cols: bfloat16 [14, 21], replicated, may hold values from -1.25 to 1.25
- basis_order: int32 [14], replicated, may hold values from 0 to 2
Outputs:
- difference: bfloat16 [512, 48, 128], P(('groups', 'patch', 'ccd')), parts along dimension 0
The draws below stay inside these ranges and needn't reach their ends.
There are 2 independent parts, one for each index of `groups`. The reference program is written for one: setup_inputs(seed, part) draws one part's arguments, and reference() takes and returns one part's arrays. A program takes and returns all parts, laid end to end along the dimension named above; an argument that names none is the same for every part. Nothing has to cross between parts.
Inputs may be any that keep to these rules, and one draw needn't show every extreme that they name: `strip_patch`: no more than 8 of one device's 16 strips intersect one patch, and in every draw some patch receives exactly 8 strips from every device.
All inputs are finite; a program needn't handle non-finite values.
Results may differ from the reference program's by a relative error of at most 0.0022.
Values may be sent and summed in bfloat16 or wider, within the bound.
No kernel may reach another device: no remote copies, remote signals or barrier semaphores. Data moves between devices by JAX's collectives and lax.ppermute only.
A program may use at most 128 MiB of HBM per device.

```python
import jax
import jax.numpy as jnp
import numpy as np
from jax import lax

ROWS = 48
COLS = 128
MARGIN = 16
TROWS = 80
KSIZE = 21
NB = 14
STRIPS_DEV = 16
TILE_DEV = 16
PATCH_ROWS = 4000
CAP = 8
STRIPS = 256
TILES = 256
N_PATCH = 4
N_CCD = 4


def strip_layout(key):
    device_total = N_PATCH * N_CCD
    slot_count = N_PATCH * CAP
    favored = jax.random.randint(jax.random.fold_in(key, 11), (), 0, N_PATCH)
    device_keys = jax.random.split(jax.random.fold_in(key, 12), device_total)
    slot_patch = jnp.arange(slot_count, dtype=jnp.int32) // CAP

    def one_device(device_key):
        shuffled = jax.random.permutation(device_key, slot_count).astype(jnp.int32)
        scores = shuffled + slot_count * (slot_patch == favored).astype(jnp.int32)
        unused, picked = lax.top_k(scores, STRIPS_DEV)
        chosen = slot_patch[picked]
        return chosen[jax.random.permutation(jax.random.fold_in(device_key, 1), STRIPS_DEV)]
    patch_ids = jax.vmap(one_device)(device_keys).reshape(-1).astype(jnp.int32)
    tile_ids = jax.random.randint(jax.random.fold_in(key, 13), (STRIPS,), 0, TILE_DEV)
    offsets = jax.random.randint(jax.random.fold_in(key, 14), (STRIPS,), 0, PATCH_ROWS - ROWS + 1)
    return (patch_ids, tile_ids, offsets)


def template_values(key):
    shape = (TILES, TROWS, COLS)
    return jax.random.normal(jax.random.fold_in(key, 21), shape, jnp.float32)


def draw_template(key, part):
    return template_values(key).astype(jnp.bfloat16)


def draw_strip_patch(key, part):
    return strip_layout(key)[0]


def draw_strip_tile(key, part):
    return strip_layout(key)[1]


def draw_strip_row(key, part):
    return strip_layout(key)[2]


def draw_science(key, part):
    patch_ids, tile_ids, offsets = strip_layout(key)
    plates = template_values(key)
    reader = jnp.arange(STRIPS, dtype=jnp.int32) // STRIPS_DEV
    ccd_index = reader % N_CCD
    patch_index = reader // N_CCD
    source = (patch_ids * N_CCD + ccd_index) * TILE_DEV + tile_ids
    chosen = plates[source]
    centre = chosen[:, MARGIN:MARGIN + ROWS]
    above = chosen[:, MARGIN - 1:MARGIN - 1 + ROWS]
    below = chosen[:, MARGIN + 1:MARGIN + 1 + ROWS]
    vertical = 0.5 * centre + 0.25 * (above + below)
    padded = jnp.pad(vertical, ((0, 0), (0, 0), (1, 1)))
    blurred = 0.5 * vertical + 0.25 * (padded[:, :, :-2] + padded[:, :, 2:])
    place = (2 * offsets + ROWS).astype(jnp.float32) / PATCH_ROWS - 1.0
    gain = (0.3 + 0.5 * ccd_index.astype(jnp.float32) / max(N_CCD - 1, 1) + 0.5 * patch_index.astype(jnp.float32) / max(N_PATCH - 1, 1)) * (1.0 + 0.3 * place)
    shape = (STRIPS, ROWS, COLS)
    noise = 0.3 * jax.random.normal(jax.random.fold_in(key, 31), shape, jnp.float32)
    result = gain[:, None, None] * blurred + 0.4 * place[:, None, None] + noise
    return result.astype(jnp.bfloat16)


def plant(drawn, stream_key, smallest, largest):
    longest = drawn.shape.index(max(drawn.shape))
    spots = []
    for shift in (0, 1):
        where = [jax.random.randint(jax.random.fold_in(stream_key, axis), (), 0, length) for axis, length in enumerate(drawn.shape)]
        where[longest] = (where[longest] + shift) % drawn.shape[longest]
        spots.append(tuple(where))
    return drawn.at[spots[0]].set(smallest).at[spots[1]].set(largest)


def scatter_about(rng, shape, spread, bound, kind=jnp.bfloat16):
    return jnp.clip(spread * jax.random.normal(rng, shape, jnp.float32), -bound, bound).astype(kind)


def setup_inputs(seed: int = 0, part: int = 0) -> dict:
    arg_keys = jax.random.split(jax.random.key(seed), 10)
    part_keys = jax.random.split(jax.random.fold_in(arg_keys[9], part), 10)
    return {
        "science": draw_science(jax.random.fold_in(jax.random.fold_in(arg_keys[9], part), 71), part),
        "strip_patch": draw_strip_patch(jax.random.fold_in(jax.random.fold_in(arg_keys[9], part), 71), part),
        "strip_tile": draw_strip_tile(jax.random.fold_in(jax.random.fold_in(arg_keys[9], part), 71), part),
        "strip_row": draw_strip_row(jax.random.fold_in(jax.random.fold_in(arg_keys[9], part), 71), part),
        "row_count": plant(jax.random.randint(part_keys[4], (STRIPS,), ROWS // 2, ROWS + 1), jax.random.fold_in(part_keys[4], 1), ROWS // 2, ROWS).astype(jnp.int32),
        "template": draw_template(jax.random.fold_in(jax.random.fold_in(arg_keys[9], part), 71), part),
        "basis_rows": scatter_about(arg_keys[6], (NB, KSIZE), KSIZE ** -0.5, 1.25),
        "basis_cols": scatter_about(arg_keys[7], (NB, KSIZE), KSIZE ** -0.5, 1.25),
        "basis_order": plant(jax.random.randint(arg_keys[8], (NB,), 0, 3), jax.random.fold_in(arg_keys[8], 1), 0, 2).astype(jnp.int32),
    }


term_powers = ((0, 0), (1, 0), (0, 1), (2, 0), (1, 1), (0, 2))
ridge_weight = 0.01
highest = lax.Precision.HIGHEST

def kernel_tables(basis_rows, basis_cols, strip_rows, tile_rows, columns):
    kernels, kernel_taps = basis_rows.shape
    middle = kernel_taps // 2
    margin = (tile_rows - strip_rows) // 2
    row_lag = jnp.arange(tile_rows)[None, :] - jnp.arange(strip_rows)[:, None] - margin + middle
    col_lag = jnp.arange(columns)[:, None] - jnp.arange(columns)[None, :] + middle
    row_table = jnp.zeros((kernels, strip_rows, tile_rows), jnp.float32)
    col_table = jnp.zeros((kernels, columns, columns), jnp.float32)
    for tap_index in range(kernel_taps):
        row_table = row_table + jnp.where((row_lag == tap_index)[None], basis_rows[:, tap_index].astype(jnp.float32)[:, None, None], 0.0)
        col_table = col_table + jnp.where((col_lag == tap_index)[None], basis_cols[:, tap_index].astype(jnp.float32)[:, None, None], 0.0)
    return (row_table.astype(jnp.bfloat16).reshape(kernels * strip_rows, tile_rows), col_table.astype(jnp.bfloat16))

def convolve(tile_stack, row_table, col_table):
    kernels = col_table.shape[0]
    columns = col_table.shape[1]
    strip_rows = row_table.shape[0] // kernels
    smoothed = jnp.einsum('ht,btc->bhc', row_table.astype(jnp.float32), tile_stack.astype(jnp.float32), precision=highest).astype(jnp.bfloat16)
    smoothed = smoothed.reshape(tile_stack.shape[0], kernels, strip_rows, columns)
    return jnp.einsum('bnrc,ncd->bnrd', smoothed.astype(jnp.float32), col_table.astype(jnp.float32), precision=highest).astype(jnp.bfloat16)

def with_ones(convolved):
    ones_plane = jnp.ones(convolved.shape[:1] + (1,) + convolved.shape[2:], jnp.bfloat16)
    return jnp.concatenate([convolved, ones_plane], axis=1)

def positions(offsets, row_totals, occupied, strip_rows, columns):
    row_steps = jnp.arange(strip_rows, dtype=jnp.int32)
    vertical = (2 * (offsets[:, None] + row_steps[None, :]) + 1).astype(jnp.float32) / PATCH_ROWS - 1.0
    across = (2 * jnp.arange(columns, dtype=jnp.int32) + 1).astype(jnp.float32) / columns - 1.0
    usable = ((row_steps[None, :] < row_totals[:, None]) & (occupied[:, None] > 0)).astype(jnp.float32)
    return (vertical, across, usable)

def strip_stats(image_stack, science, vertical, across, usable):
    strips_here, plane_count, strip_rows, columns = image_stack.shape
    across_powers = jnp.stack([across ** degree for degree in range(5)])
    scaled = (across_powers[None, :, None, None, :] * image_stack[:, None].astype(jnp.float32)).astype(jnp.bfloat16)
    scaled = scaled.reshape(strips_here, 5 * plane_count, strip_rows, columns)
    row_mask = usable.astype(jnp.bfloat16)
    weighted = jnp.concatenate([image_stack * row_mask[:, None, :, None], (science * row_mask[:, :, None])[:, None]], axis=1)
    products = jnp.einsum('bxrc,bkrc->brxk', scaled.astype(jnp.float32), weighted.astype(jnp.float32), precision=highest)
    vertical_powers = jnp.stack([vertical ** degree for degree in range(5)], axis=1)
    return jnp.einsum('bar,brxk->baxk', vertical_powers, products, precision=highest)

def solve_patch(moments, basis_order):
    plane_count = moments.shape[2] - 1
    kernels = plane_count - 1
    term_count = len(term_powers)
    unknowns = term_count * plane_count
    term_of = np.arange(unknowns) // plane_count
    plane_of = np.arange(unknowns) % plane_count
    first_power = np.array([term_powers[entry][0] for entry in term_of])
    second_power = np.array([term_powers[entry][1] for entry in term_of])
    pair_up = first_power[:, None] + first_power[None, :]
    pair_side = second_power[:, None] + second_power[None, :]
    row_planes = np.broadcast_to(plane_of[:, None], (unknowns, unknowns))
    col_planes = np.broadcast_to(plane_of[None, :], (unknowns, unknowns))
    paired = moments[pair_up, pair_side * plane_count + row_planes, col_planes]
    normal = 0.5 * (paired + paired.T)
    target = moments[first_power, second_power * plane_count + plane_of, plane_count]
    degree_of = first_power + second_power
    selector = plane_of[:, None] == np.arange(kernels)[None, :]
    order_of = jnp.sum(jnp.where(selector, basis_order[None, :], 0), axis=1)
    active = jnp.where(plane_of == kernels, 1.0, (degree_of <= order_of).astype(jnp.float32))
    system = active[:, None] * active[None, :] * normal + jnp.diag(1.0 + ridge_weight * active * jnp.diagonal(normal))
    factor = jnp.linalg.cholesky(system)
    halfway = lax.linalg.triangular_solve(factor, (active * target)[:, None], left_side=True, lower=True)
    solved = lax.linalg.triangular_solve(factor, halfway, left_side=True, lower=True, transpose_a=True)
    return solved[:, 0].reshape(term_count, plane_count)

def strip_model(image_stack, science, vertical, across, usable, coefficients):
    term_maps = jnp.stack([vertical[:, :, None] ** up_power * across[None, None, :] ** side_power for up_power, side_power in term_powers], axis=1)
    weights_map = jnp.einsum('bjn,bjrc->bnrc', coefficients, term_maps, precision=highest)
    fitted = jnp.sum(weights_map * image_stack.astype(jnp.float32), axis=1)
    return (usable[:, :, None] * (science.astype(jnp.float32) - fitted)).astype(jnp.bfloat16)

def block_stats(tile_stack, science, offsets, row_totals, occupied, tables):
    image_stack = with_ones(convolve(tile_stack, tables[0], tables[1]))
    vertical, across, usable = positions(offsets, row_totals, occupied, science.shape[1], science.shape[2])
    return strip_stats(image_stack, science, vertical, across, usable)

def block_model(tile_stack, science, offsets, row_totals, occupied, tables, coefficients):
    image_stack = with_ones(convolve(tile_stack, tables[0], tables[1]))
    vertical, across, usable = positions(offsets, row_totals, occupied, science.shape[1], science.shape[2])
    return strip_model(image_stack, science, vertical, across, usable, coefficients)

def reference(science, strip_patch, strip_tile, strip_row, row_count, template, basis_rows, basis_cols, basis_order):
    strip_total, strip_rows, columns = science.shape
    tile_rows = template.shape[1]
    plane_count = basis_rows.shape[0] + 1
    tables = kernel_tables(basis_rows, basis_cols, strip_rows, tile_rows, columns)
    reader = jnp.arange(strip_total, dtype=jnp.int32) // STRIPS_DEV
    tile_index = ((strip_patch * N_CCD + reader % N_CCD) * TILE_DEV + strip_tile).astype(jnp.int32)
    owner_hot = (strip_patch[:, None] == jnp.arange(N_PATCH, dtype=jnp.int32)[None, :]).astype(jnp.float32)
    block_size = 16
    blocks = strip_total // block_size

    def in_blocks(source):
        return source.reshape((blocks, block_size) + source.shape[1:])
    pieces = (in_blocks(tile_index), in_blocks(science), in_blocks(strip_row), in_blocks(row_count), in_blocks(owner_hot))
    present = jnp.ones((block_size,), jnp.int32)

    def add_stats(totals, block_data):
        indices, images, offsets, row_totals, hot_rows = block_data
        moments = block_stats(template[indices], images, offsets, row_totals, present, tables)
        return (totals + jnp.einsum('bq,baxk->qaxk', hot_rows, moments, precision=highest), jnp.zeros((), jnp.float32))
    start_totals = jnp.zeros((N_PATCH, 5, 5 * plane_count, plane_count + 1), jnp.float32)
    totals, unused = lax.scan(add_stats, start_totals, pieces)
    solved = jax.vmap(solve_patch, in_axes=(0, None))(totals, basis_order)

    def difference_step(carry, block_data):
        indices, images, offsets, row_totals, hot_rows = block_data
        strip_coefficients = jnp.einsum('sq,qjn->sjn', hot_rows, solved, precision=highest)
        return (carry, block_model(template[indices], images, offsets, row_totals, present, tables, strip_coefficients))
    carried, outputs = lax.scan(difference_step, jnp.zeros((), jnp.float32), pieces)
    return outputs.reshape(strip_total, strip_rows, columns)
```

```python
import functools

import jax
import jax.numpy as jnp
from jax import lax
from jax.experimental import pallas as pl
from jax.experimental.pallas import tpu as pltpu
from jax.sharding import PartitionSpec as P

PATCH_ROWS = 4000
RIDGE = 0.01
TERMS = ((0, 0), (2, 0), (0, 2), (1, 0), (0, 1), (1, 1))
LEFT = 3
BATCH = 4
VMEM = pl.BlockSpec(memory_space=pltpu.VMEM)
SMEM = pl.BlockSpec(memory_space=pltpu.SMEM)
F32, BF16, I32 = jnp.float32, jnp.bfloat16, jnp.int32


def block_of(a, b):
    want = (TERMS[a][0] + TERMS[b][0], TERMS[a][1] + TERMS[b][1])
    for left in range(LEFT):
        for right in range(len(TERMS)):
            if (TERMS[left][0] + TERMS[right][0], TERMS[left][1] + TERMS[right][1]) == want:
                return left, right
    raise ValueError(want)


def params():
    return pltpu.CompilerParams(vmem_limit_bytes=56 * 1024 * 1024)


def tables_kernel(rows_ref, cols_ref, row_out, col_out, *, kernels, taps, rows, tile_rows, columns):
    middle = taps // 2
    lag = (tile_rows - rows) // 2 - middle
    cc = lax.broadcasted_iota(I32, (columns, columns), 0)
    dd = lax.broadcasted_iota(I32, (columns, columns), 1)
    band = (cc - dd <= middle) & (dd - cc <= middle)
    for n in range(kernels):
        taps_n = jnp.broadcast_to(rows_ref[n : n + 1, :], (rows, 128))
        moved = pltpu.roll(taps_n, lag, 1, stride=1, stride_axis=0)
        row_out[n * rows : (n + 1) * rows, :] = moved[:, :tile_rows].astype(BF16)
        taps_n = jnp.broadcast_to(cols_ref[n : n + 1, :], (columns, columns))
        moved = pltpu.roll(taps_n, 0, 1, stride=1, stride_axis=0)
        col_out[n] = jnp.where(band, moved, 0.0).astype(BF16)


def make_tables(basis_rows, basis_cols, rows, tile_rows, columns):
    kernels, taps = basis_rows.shape
    pad = ((0, 0), (0, 128 - taps))
    return pl.pallas_call(
        functools.partial(
            tables_kernel,
            kernels=kernels,
            taps=taps,
            rows=rows,
            tile_rows=tile_rows,
            columns=columns,
        ),
        out_shape=(
            jax.ShapeDtypeStruct((kernels * rows, tile_rows), BF16),
            jax.ShapeDtypeStruct((kernels, columns, columns), BF16),
        ),
        in_specs=[VMEM, VMEM],
        out_specs=(VMEM, VMEM),
        compiler_params=params(),
        name="tables",
    )(
        jnp.pad(basis_rows.astype(F32), pad),
        jnp.roll(jnp.pad(basis_cols.astype(F32)[:, ::-1], pad), -(taps // 2), axis=1),
    )


def select_kernel(me_ref, *refs, shifts, strips, tiles):
    codes, template, outs = refs[:shifts], refs[shifts], refs[shifts + 1 :]
    low = me_ref[0] * tiles
    for code_ref, out in zip(codes, outs):

        def step(s, count, code_ref=code_ref, out=out):
            tile = code_ref[s] - low
            hit = (tile >= 0) & (tile < tiles)

            @pl.when(hit)
            def _():
                out[count] = template[tile]

            return count + hit.astype(I32)

        lax.fori_loop(0, strips, step, jnp.int32(0))


def select_tiles(me, codes, template, capacity):
    shifts = len(codes)
    tiles, tile_rows, columns = template.shape
    return pl.pallas_call(
        functools.partial(select_kernel, shifts=shifts, strips=codes[0].shape[0], tiles=tiles),
        out_shape=[jax.ShapeDtypeStruct((capacity, tile_rows, columns), BF16)] * shifts,
        in_specs=[SMEM] + [SMEM] * shifts + [VMEM],
        out_specs=[VMEM] * shifts,
        compiler_params=params(),
        name="select",
    )(me, *codes, template)


def list_group(code_ref, listing, patch, tiles, strips):
    low = patch * tiles

    def step(s, count):
        tile = code_ref[s] - low
        hit = (tile >= 0) & (tile < tiles)

        @pl.when(hit)
        def _():
            listing[count] = s

        return count + hit.astype(I32)

    return lax.fori_loop(0, strips, step, jnp.int32(0))


def across_rows(columns):
    c = lax.broadcasted_iota(I32, (8, columns), 1)
    return (2 * c + 1).astype(F32) / columns - 1.0


def moments_kernel(
    me_ref,
    code_ref,
    row_ref,
    good_ref,
    plates,
    science,
    row_table,
    col_table,
    *refs,
    first,
    groups,
    capacity,
    own,
    patches,
    ccds,
    share,
    kernels,
    planes,
    earlier,
):
    before = refs[:earlier]
    outs = refs[earlier : len(refs) - 3]
    p32, listing, sums = refs[len(refs) - 3 :]
    last = len(outs) > 2
    planes_out = outs[0]
    strips, rows, columns = science.shape
    tiles = me_ref[2]
    me, ccd = me_ref[0], me_ref[1]
    span = rows * planes
    unknowns = len(TERMS) * planes
    if kernels + 2 < planes:
        p32[...] = jnp.zeros_like(p32)
    for b in range(BATCH):
        p32[pl.ds(b * span + kernels, rows, stride=planes), :] = jnp.ones((rows, columns), F32)
    across = jnp.concatenate([across_rows(columns)] * (planes // 8), axis=0)
    across2 = across * across
    step_rows = 8

    def gram(b, strip, slot):
        offset = row_ref[strip]
        good = good_ref[strip]
        total = jnp.zeros((LEFT * planes, unknowns), F32)
        for chunk in range(rows // step_rows):
            pieces = [[] for _ in TERMS]
            for r in range(chunk * step_rows, (chunk + 1) * step_rows):
                at = r * planes
                rounded = p32[b * span + at : b * span + at + planes, :].astype(BF16)
                planes_out[slot, at : at + planes, :] = rounded
                value = rounded.astype(F32)
                v = (2 * (offset + r) + 1).astype(F32) * (1.0 / PATCH_ROWS) - 1.0
                value = value * jnp.where(r < good, 1.0, 0.0)
                with_u = value * across
                pieces[0].append(value.astype(BF16))
                pieces[1].append((value * (v * v)).astype(BF16))
                pieces[2].append((value * across2).astype(BF16))
                pieces[3].append((value * v).astype(BF16))
                pieces[4].append(with_u.astype(BF16))
                pieces[5].append((with_u * v).astype(BF16))
            wide = [jnp.concatenate(part, axis=1) for part in pieces]
            right = jnp.concatenate(wide, axis=0)
            left = jnp.concatenate(wide[:LEFT], axis=0)
            total = total + lax.dot_general(
                left, right, (((1,), (1,)), ((), ())), preferred_element_type=F32
            )
        return total

    def group(g, carry):
        patch = me + (first + g)
        patch = jnp.where(patch >= patches, patch - patches, patch)
        count = list_group(code_ref, listing, patch, tiles, strips)
        sums[first + g] = jnp.zeros((LEFT * planes, 128), F32)

        def batch(t, carry):
            slots = [t * BATCH + b for b in range(BATCH)]
            chosen = [listing[jnp.minimum(slot, count - 1)] for slot in slots]
            if own:
                stack = [plates[code_ref[s] - patch * tiles] for s in chosen]
            else:
                stack = [plates[g * capacity + jnp.minimum(slot, count - 1)] for slot in slots]
            smoothed = jnp.dot(
                row_table[...], jnp.concatenate(stack, axis=1), preferred_element_type=F32
            ).astype(BF16)
            for n in range(kernels):
                part = smoothed[n * rows : (n + 1) * rows]
                lhs = jnp.concatenate(
                    [part[:, b * columns : (b + 1) * columns] for b in range(BATCH)], axis=0
                )
                convolved = jnp.dot(lhs, col_table[n], preferred_element_type=F32)
                for b in range(BATCH):
                    p32[pl.ds(b * span + n, rows, stride=planes), :] = convolved[
                        b * rows : (b + 1) * rows
                    ]
            for b in range(BATCH):
                p32[pl.ds(b * span + planes - 1, rows, stride=planes), :] = science[
                    chosen[b]
                ].astype(F32)
            for b in range(BATCH):

                @pl.when(slots[b] < count)
                def _(b=b):
                    total = gram(b, chosen[b], g * capacity + slots[b])
                    sums[first + g, :, :unknowns] += total

            return carry

        lax.fori_loop(0, (count + BATCH - 1) // BATCH, batch, 0)
        return carry

    if groups == 1:
        group(0, 0)
    else:
        lax.fori_loop(0, groups, group, 0)
    if not last:
        outs[1][...] = sums[first : first + groups]
    else:
        at = 0
        for ref in before:
            for i in range(ref.shape[0]):
                sums[at] = ref[i]
                at += 1
        for e in range(ccds):
            owner = ccd + e
            owner = jnp.where(owner >= ccds, owner - ccds, owner)
            for k in range(share):
                d = jnp.minimum(k * ccds + owner, patches - 1) - me
                d = jnp.where(d < 0, d + patches, d)
                outs[1 + e][k] = sums[d]


def moments_call(scalars, plates, science, tables, before, first, groups, own, last, sizes):
    capacity, patches, ccds, share, kernels, planes = sizes
    strips, rows, columns = science.shape
    held = groups * capacity
    sum_shape = (LEFT * planes, 128)
    if last:
        sum_outs = [jax.ShapeDtypeStruct((share,) + sum_shape, F32)] * ccds
    else:
        sum_outs = [jax.ShapeDtypeStruct((groups,) + sum_shape, F32)]
    return pl.pallas_call(
        functools.partial(
            moments_kernel,
            first=first,
            groups=groups,
            capacity=capacity,
            own=own,
            patches=patches,
            ccds=ccds,
            share=share,
            kernels=kernels,
            planes=planes,
            earlier=len(before),
        ),
        out_shape=[jax.ShapeDtypeStruct((held, rows * planes, columns), BF16)] + sum_outs,
        in_specs=[SMEM] * 4 + [VMEM] * (4 + len(before)),
        out_specs=[VMEM] * (1 + len(sum_outs)),
        scratch_shapes=[
            pltpu.VMEM((BATCH * rows * planes, columns), F32),
            pltpu.SMEM((strips,), I32),
            pltpu.VMEM((max(patches, ccds),) + sum_shape, F32),
        ],
        compiler_params=params(),
        cost_estimate=pl.CostEstimate(
            flops=int(4e9) * groups // patches, bytes_accessed=1 << 20, transcendentals=0
        ),
        name="moments",
    )(*scalars, plates, science, *tables, *before)


def solve_kernel(order_ref, *refs, kernels, planes, share):
    parts, out = refs[:-1], refs[-1]
    terms = len(TERMS)
    size = terms * planes
    lane = lax.broadcasted_iota(I32, (size, 128), 1)
    sub = lax.broadcasted_iota(I32, (size, 128), 0)

    def activity(index):
        plane, term = index % planes, index // planes
        order = jnp.zeros_like(index)
        for i in range(kernels):
            order = jnp.where(plane == i, order_ref[i], order)
        degree = jnp.zeros_like(index)
        for t, powers in enumerate(TERMS):
            degree = jnp.where(term == t, powers[0] + powers[1], degree)
        wanted = (plane == kernels) | ((plane < kernels) & (degree <= order))
        return jnp.where(wanted & (index < size), 1.0, 0.0)

    active_row = activity(lane[:8])
    active_row = jnp.concatenate([active_row] * (size // 8), axis=0)
    active_col = activity(sub)
    lane16 = lane[:planes]
    row8 = lax.broadcasted_iota(I32, (8, 128), 0)
    for k in range(share):
        moments = parts[0][k]
        for ref in parts[1:]:
            moments = moments + ref[k]
        rows = []
        for a in range(terms):
            row = jnp.zeros((planes, 128), F32)
            for b in range(terms):
                left, right = block_of(a, b)
                piece = moments[left * planes : (left + 1) * planes]
                if b != right:
                    piece = pltpu.roll(piece, ((b - right) * planes) % 128, 1)
                row = jnp.where(lane16 // planes == b, piece, row)
            rows.append(row)
        paired = jnp.concatenate(rows, axis=0)
        target = pltpu.roll(paired, size - (planes - 1), 1)
        masked = active_row * active_col * paired
        system = jnp.where(lane == sub, masked + (1.0 + RIDGE * masked), masked)
        system = jnp.where(lane == size, active_col * target, system)
        blocks = [system[8 * m : 8 * m + 8] for m in range(size // 8)]
        for x in range(size):
            if x % planes > kernels:
                continue
            at, inner = divmod(x, 8)
            row = jnp.broadcast_to(blocks[at][inner : inner + 1], (8, 128))
            pivot = jnp.broadcast_to(row[:, x : x + 1], (8, 128))
            scaled = row * (1.0 / pivot)
            for m in range(size // 8):
                column = jnp.broadcast_to(blocks[m][:, x : x + 1], (8, 128))
                new = blocks[m] - column * scaled
                if m == at:
                    new = jnp.where(row8 == inner, scaled, new)
                blocks[m] = new
        answer = jnp.concatenate(blocks, axis=0)
        answer = jnp.broadcast_to(answer[:, size : size + 1], (size, 128))
        answer = jnp.where(sub % planes == lane % planes, answer, 0.0)
        lines = [
            jnp.sum(answer[t * planes : (t + 1) * planes], axis=0, keepdims=True)
            for t in range(terms)
        ]
        lines.append(jnp.zeros((8 - terms, 128), F32))
        out[k] = jnp.concatenate(lines, axis=0)


def solve(order, parts, kernels, planes):
    share = parts[0].shape[0]
    return pl.pallas_call(
        functools.partial(solve_kernel, kernels=kernels, planes=planes, share=share),
        out_shape=jax.ShapeDtypeStruct((share, 8, 128), F32),
        in_specs=[SMEM] + [VMEM] * len(parts),
        out_specs=VMEM,
        compiler_params=params(),
        name="solve",
    )(order, *parts)


def difference_kernel(
    me_ref,
    code_ref,
    row_ref,
    good_ref,
    *refs,
    calls,
    capacity,
    patches,
    ccds,
    share,
    kernels,
    planes,
    tall,
):
    coefs, stacks = refs[:ccds], refs[ccds : ccds + len(calls)]
    out, table, listing = refs[ccds + len(calls) :]
    strips, rows, columns = out.shape
    me, ccd, tiles = me_ref[0], me_ref[1], me_ref[2]
    for e in range(ccds):
        owner = ccd + e
        owner = jnp.where(owner >= ccds, owner - ccds, owner)
        for k in range(share):
            table[k * ccds + owner] = coefs[e][k]
    across = jnp.concatenate([across_rows(columns)] * (tall // 8), axis=0)
    across2 = across * across
    width = tall * planes
    lane = lax.broadcasted_iota(I32, (tall, width), 1)
    sub = lax.broadcasted_iota(I32, (tall, width), 0)
    diagonal = lane // planes == sub
    is_science = diagonal & (lane % planes == planes - 1)
    sub_out = lax.broadcasted_iota(I32, (tall, columns), 0)

    def pieces(value):
        high = value.astype(BF16)
        rest = value - high.astype(F32)
        middle = rest.astype(BF16)
        return high, middle, (rest - middle.astype(F32)).astype(BF16)

    for (first, groups), stack in zip(calls, stacks):

        def group(g, carry, first=first, stack=stack):
            patch = me + (first + g)
            patch = jnp.where(patch >= patches, patch - patches, patch)
            count = list_group(code_ref, listing, patch, tiles, strips)
            block = table[patch]
            coef = [
                jnp.broadcast_to(
                    jnp.concatenate([block[t : t + 1]] * (width // 128), axis=1), (tall, width)
                )
                for t in range(len(TERMS))
            ]

            def strip_step(j, carry):
                strip = listing[j]
                offset, good = row_ref[strip], good_ref[strip]
                for h in range(rows // tall):
                    v = (2 * (offset + h * tall + sub) + 1).astype(F32) / PATCH_ROWS - 1.0
                    plain = coef[0] + v * (coef[3] + v * coef[1])
                    once = coef[4] + v * coef[5]
                    twice = coef[2]
                    plain = jnp.where(diagonal, -plain, 0.0)
                    plain = jnp.where(is_science, 1.0, plain)
                    once = jnp.where(diagonal, -once, 0.0)
                    twice = jnp.where(diagonal, -twice, 0.0)
                    lhs = jnp.concatenate([*pieces(plain), *pieces(once), *pieces(twice)], axis=0)
                    rhs = stack[g * capacity + j, h * width : (h + 1) * width, :]
                    got = jnp.dot(lhs, rhs, preferred_element_type=F32)
                    part = [got[i * tall : (i + 1) * tall] for i in range(9)]
                    value = (
                        (part[0] + (part[1] + part[2]))
                        + across * (part[3] + (part[4] + part[5]))
                        + across2 * (part[6] + (part[7] + part[8]))
                    )
                    value = jnp.where(h * tall + sub_out < good, value, 0.0)
                    out[strip, h * tall : (h + 1) * tall, :] = value.astype(BF16)
                return carry

            lax.fori_loop(0, count, strip_step, 0)
            return carry

        if groups == 1:
            group(0, 0)
        else:
            lax.fori_loop(0, groups, group, 0)


def difference(scalars, coefs, stacks, calls, shape, sizes):
    capacity, patches, ccds, share, kernels, planes = sizes
    strips, rows, columns = shape
    return pl.pallas_call(
        functools.partial(
            difference_kernel,
            calls=calls,
            capacity=capacity,
            patches=patches,
            ccds=ccds,
            share=share,
            kernels=kernels,
            planes=planes,
            tall=16,
        ),
        out_shape=jax.ShapeDtypeStruct(shape, BF16),
        in_specs=[SMEM] * 4 + [VMEM] * (len(coefs) + len(stacks)),
        out_specs=VMEM,
        scratch_shapes=[
            pltpu.VMEM((share * ccds, 8, 128), F32),
            pltpu.SMEM((strips,), I32),
        ],
        compiler_params=params(),
        name="difference",
    )(*scalars, *coefs, *stacks)


def shifted(value, axis, shift):
    size = lax.axis_size(axis)
    return lax.ppermute(value, axis, [(i, (i + shift) % size) for i in range(size)])


def body(
    science,
    strip_patch,
    strip_tile,
    strip_row,
    row_count,
    template,
    basis_rows,
    basis_cols,
    basis_order,
):
    patches, ccds = lax.axis_size("patch"), lax.axis_size("ccd")
    strips, rows, columns = science.shape
    tiles, tile_rows = template.shape[:2]
    kernels = basis_rows.shape[0]
    planes = -(-(kernels + 2) // 16) * 16
    capacity = max(2, 2 * strips // patches)
    share = -(-patches // ccds)
    sizes = (capacity, patches, ccds, share, kernels, planes)
    me = jnp.stack(
        [lax.axis_index("patch"), lax.axis_index("ccd"), jnp.int32(tiles)]
    ).astype(I32)
    code = strip_patch * tiles + strip_tile
    scalars = (me, code, strip_row, row_count)
    if patches <= 8:
        codes = [shifted(code, "patch", d) for d in range(1, patches)]
    else:
        everyone = lax.all_gather(code, "patch")
        mine = lax.axis_index("patch")
        codes = [
            lax.dynamic_index_in_dim(
                everyone, lax.rem(mine - d + patches, patches), 0, keepdims=False
            )
            for d in range(1, patches)
        ]
    tables = make_tables(basis_rows, basis_cols, rows, tile_rows, columns)
    chosen = select_tiles(me, codes, template, capacity)
    arrived = [shifted(tile, "patch", patches - d) for d, tile in enumerate(chosen, 1)]
    if patches <= 8:
        calls = [(d, 1) for d in range(patches)]
        plates = [template] + arrived
    else:
        calls = [(0, 1), (1, patches - 1)]
        plates = [template, jnp.concatenate(arrived, axis=0)]
    stacks, sums = [], []
    for (first, groups), plate in zip(calls, plates):
        last = first + groups == patches
        got = moments_call(
            scalars, plate, science, tables, sums if last else [], first, groups, first == 0, last,
            sizes,
        )
        stacks.append(got[0])
        if not last:
            sums.append(got[1])
        else:
            scattered = got[1:]
    mine = scattered[0]
    for e in range(1, ccds):
        mine = mine + shifted(scattered[e], "ccd", e)
    parts = [mine] + [shifted(mine, "patch", d) for d in range(1, patches)]
    coefficients = solve(basis_order, parts, kernels, planes)
    coefs = [coefficients] + [shifted(coefficients, "ccd", ccds - e) for e in range(1, ccds)]
    return difference(scalars, coefs, stacks, tuple(calls), science.shape, sizes)


def solution(mesh):
    spread = P(("groups", "patch", "ccd"))
    return jax.shard_map(
        body,
        mesh=mesh,
        in_specs=(spread,) * 6 + (P(), P(), P()),
        out_specs=spread,
        check_vma=False,
    )
```

```python
import functools

import jax
import jax.numpy as jnp
from jax import lax
from jax.experimental import pallas as pl
from jax.experimental.pallas import tpu as pltpu
from jax.sharding import PartitionSpec as P

PATCH_ROWS = 4000
RIDGE = 0.01
TERMS = ((0, 0), (2, 0), (0, 2), (1, 0), (0, 1), (1, 1))
LEFT = 3
BATCH = 4
PAIR = 2
VMEM = pl.BlockSpec(memory_space=pltpu.VMEM)
SMEM = pl.BlockSpec(memory_space=pltpu.SMEM)
F32, BF16, I32 = jnp.float32, jnp.bfloat16, jnp.int32


def block_of(a, b):
    want = (TERMS[a][0] + TERMS[b][0], TERMS[a][1] + TERMS[b][1])
    for left in range(LEFT):
        for right in range(len(TERMS)):
            if (TERMS[left][0] + TERMS[right][0], TERMS[left][1] + TERMS[right][1]) == want:
                return left, right
    raise ValueError(want)


def params(mebibytes):
    return pltpu.CompilerParams(vmem_limit_bytes=mebibytes * 1024 * 1024)


def tables_kernel(rows_ref, cols_ref, row_out, col_out, *, kernels, taps, rows, tile_rows, columns):
    middle = taps // 2
    lag = (tile_rows - rows) // 2 - middle
    cc = lax.broadcasted_iota(I32, (columns, columns), 0)
    dd = lax.broadcasted_iota(I32, (columns, columns), 1)
    band = (cc - dd <= middle) & (dd - cc <= middle)
    for n in range(kernels):
        taps_n = jnp.broadcast_to(rows_ref[n : n + 1, :], (rows, 128))
        moved = pltpu.roll(taps_n, lag, 1, stride=1, stride_axis=0)
        row_out[n * rows : (n + 1) * rows, :] = moved[:, :tile_rows].astype(BF16)
        taps_n = jnp.broadcast_to(cols_ref[n : n + 1, :], (columns, columns))
        moved = pltpu.roll(taps_n, 0, 1, stride=1, stride_axis=0)
        col_out[n] = jnp.where(band, moved, 0.0).astype(BF16)


def make_tables(basis_rows, basis_cols, rows, tile_rows, columns):
    kernels, taps = basis_rows.shape
    pad = ((0, 0), (0, 128 - taps))
    return pl.pallas_call(
        functools.partial(
            tables_kernel,
            kernels=kernels,
            taps=taps,
            rows=rows,
            tile_rows=tile_rows,
            columns=columns,
        ),
        out_shape=(
            jax.ShapeDtypeStruct((kernels * rows, tile_rows), BF16),
            jax.ShapeDtypeStruct((kernels, columns, columns), BF16),
        ),
        in_specs=[VMEM, VMEM],
        out_specs=(VMEM, VMEM),
        compiler_params=params(8),
        name="tables",
    )(
        jnp.pad(basis_rows.astype(F32), pad),
        jnp.roll(jnp.pad(basis_cols.astype(F32)[:, ::-1], pad), -(taps // 2), axis=1),
    )


def select_kernel(me_ref, *refs, shifts, strips, tiles):
    codes, template, outs = refs[:shifts], refs[shifts], refs[shifts + 1 :]
    low = me_ref[0] * tiles
    for code_ref, out in zip(codes, outs):

        def step(s, count, code_ref=code_ref, out=out):
            tile = code_ref[s] - low
            hit = (tile >= 0) & (tile < tiles)

            @pl.when(hit)
            def _():
                out[count] = template[tile]

            return count + hit.astype(I32)

        lax.fori_loop(0, strips, step, jnp.int32(0))


def select_tiles(me, codes, template, capacity):
    shifts = len(codes)
    tiles, tile_rows, columns = template.shape
    return pl.pallas_call(
        functools.partial(select_kernel, shifts=shifts, strips=codes[0].shape[0], tiles=tiles),
        out_shape=[jax.ShapeDtypeStruct((capacity, tile_rows, columns), BF16)] * shifts,
        in_specs=[SMEM] + [SMEM] * shifts + [VMEM],
        out_specs=[VMEM] * shifts,
        compiler_params=params(8),
        name="select",
    )(me, *codes, template)


def list_group(code_ref, listing, patch, tiles, strips):
    low = patch * tiles

    def step(s, count):
        tile = code_ref[s] - low
        hit = (tile >= 0) & (tile < tiles)

        @pl.when(hit)
        def _():
            listing[count] = s

        return count + hit.astype(I32)

    return lax.fori_loop(0, strips, step, jnp.int32(0))


def across_rows(columns):
    c = lax.broadcasted_iota(I32, (8, columns), 1)
    return (2 * c + 1).astype(F32) / columns - 1.0


def moments_kernel(
    me_ref,
    code_ref,
    row_ref,
    good_ref,
    plates,
    science,
    row_table,
    col_table,
    *refs,
    first,
    groups,
    capacity,
    own,
    patches,
    ccds,
    share,
    kernels,
    planes,
    earlier,
):
    before = refs[:earlier]
    outs = refs[earlier : len(refs) - 3]
    p32, listing, sums = refs[len(refs) - 3 :]
    last = len(outs) > 2
    planes_out = outs[0]
    strips, rows, columns = science.shape
    tiles = me_ref[2]
    me, ccd = me_ref[0], me_ref[1]
    span = rows * planes
    unknowns = len(TERMS) * planes
    if kernels + 2 < planes:
        p32[...] = jnp.zeros_like(p32)
    for b in range(BATCH):
        p32[pl.ds(b * span + kernels, rows, stride=planes), :] = jnp.ones((rows, columns), F32)
    across = jnp.concatenate([across_rows(columns)] * (planes // 8), axis=0)
    across = across.astype(BF16)
    step_rows = 8

    def gram(first_b, chosen, goods, slots):
        offsets = [row_ref[strip] for strip in chosen]
        totals = [jnp.zeros((unknowns, LEFT * planes), F32) for _ in chosen]
        for chunk in range(rows // step_rows):
            operands = []
            for i in range(len(chosen)):
                pieces = [[] for _ in TERMS]
                for r in range(chunk * step_rows, (chunk + 1) * step_rows):
                    at = r * planes
                    base = (first_b + i) * span + at
                    value = p32[base : base + planes, :].astype(BF16)
                    planes_out[slots[i], at : at + planes, :] = value
                    v = (2 * (offsets[i] + r) + 1).astype(F32) * (1.0 / PATCH_ROWS) - 1.0
                    value = value * jnp.where(r < goods[i], 1.0, 0.0).astype(BF16)
                    with_v = value.astype(F32) * v
                    with_u = value * across
                    once = with_v.astype(BF16)
                    pieces[0].append(value)
                    pieces[1].append((with_v * v).astype(BF16))
                    pieces[2].append(with_u * across)
                    pieces[3].append(once)
                    pieces[4].append(with_u)
                    pieces[5].append(once * across)
                wide = [jnp.concatenate(part, axis=1) for part in pieces]
                operands.append(
                    (jnp.concatenate(wide, axis=0), jnp.concatenate(wide[:LEFT], axis=0))
                )
            for i, (every, left) in enumerate(operands):
                totals[i] = totals[i] + lax.dot_general(
                    every, left, (((1,), (1,)), ((), ())), preferred_element_type=F32
                )
        return functools.reduce(lambda a, b: a + b, totals)

    def group(g, carry):
        patch = me + (first + g)
        patch = jnp.where(patch >= patches, patch - patches, patch)
        count = list_group(code_ref, listing, patch, tiles, strips)
        sums[first + g] = jnp.zeros((LEFT * planes, 128), F32)

        def batch(t, carry):
            slots = [t * BATCH + b for b in range(BATCH)]
            chosen = [listing[jnp.minimum(slot, count - 1)] for slot in slots]
            if own:
                stack = [plates[code_ref[s] - patch * tiles] for s in chosen]
            else:
                stack = [plates[g * capacity + jnp.minimum(slot, count - 1)] for slot in slots]
            smoothed = jnp.dot(
                row_table[...], jnp.concatenate(stack, axis=1), preferred_element_type=F32
            ).astype(BF16)
            for n in range(kernels):
                part = smoothed[n * rows : (n + 1) * rows]
                lhs = jnp.concatenate(
                    [part[:, b * columns : (b + 1) * columns] for b in range(BATCH)], axis=0
                )
                convolved = jnp.dot(lhs, col_table[n], preferred_element_type=F32)
                for b in range(BATCH):
                    p32[pl.ds(b * span + n, rows, stride=planes), :] = convolved[
                        b * rows : (b + 1) * rows
                    ]
            for b in range(BATCH):
                p32[pl.ds(b * span + planes - 1, rows, stride=planes), :] = science[
                    chosen[b]
                ].astype(F32)
            total = jnp.zeros((unknowns, LEFT * planes), F32)
            for b in range(0, BATCH, PAIR):
                these = slice(b, b + PAIR)
                goods = [
                    jnp.where(slot < count, good_ref[strip], 0)
                    for slot, strip in zip(slots[these], chosen[these])
                ]
                total = total + gram(
                    b, chosen[these], goods, [g * capacity + slot for slot in slots[these]]
                )
            half = LEFT * planes
            sums[first + g, :, :half] += total[:half]
            sums[first + g, :, half : 2 * half] += total[half:]
            return carry

        lax.fori_loop(0, (count + BATCH - 1) // BATCH, batch, 0)
        return carry

    if groups == 1:
        group(0, 0)
    else:
        lax.fori_loop(0, groups, group, 0)
    if not last:
        outs[1][...] = sums[first : first + groups]
    else:
        at = 0
        for ref in before:
            for i in range(ref.shape[0]):
                sums[at] = ref[i]
                at += 1
        for e in range(ccds):
            owner = ccd + e
            owner = jnp.where(owner >= ccds, owner - ccds, owner)
            for k in range(share):
                d = jnp.minimum(k * ccds + owner, patches - 1) - me
                d = jnp.where(d < 0, d + patches, d)
                outs[1 + e][k] = sums[d]


def moments_call(scalars, plates, science, tables, before, first, groups, own, last, sizes):
    capacity, patches, ccds, share, kernels, planes = sizes
    strips, rows, columns = science.shape
    held = groups * capacity
    sum_shape = (LEFT * planes, 128)
    if last:
        sum_outs = [jax.ShapeDtypeStruct((share,) + sum_shape, F32)] * ccds
    else:
        sum_outs = [jax.ShapeDtypeStruct((groups,) + sum_shape, F32)]
    return pl.pallas_call(
        functools.partial(
            moments_kernel,
            first=first,
            groups=groups,
            capacity=capacity,
            own=own,
            patches=patches,
            ccds=ccds,
            share=share,
            kernels=kernels,
            planes=planes,
            earlier=len(before),
        ),
        out_shape=[jax.ShapeDtypeStruct((held, rows * planes, columns), BF16)] + sum_outs,
        in_specs=[SMEM] * 4 + [VMEM] * (4 + len(before)),
        out_specs=[VMEM] * (1 + len(sum_outs)),
        scratch_shapes=[
            pltpu.VMEM((BATCH * rows * planes, columns), F32),
            pltpu.SMEM((strips,), I32),
            pltpu.VMEM((max(patches, ccds),) + sum_shape, F32),
        ],
        compiler_params=params(20),
        cost_estimate=pl.CostEstimate(
            flops=int(4e9) * groups // patches, bytes_accessed=1 << 20, transcendentals=0
        ),
        name="moments",
    )(*scalars, plates, science, *tables, *before)


def solve_kernel(order_ref, *refs, kernels, planes, share):
    parts, out = refs[:-1], refs[-1]
    terms = len(TERMS)
    size = terms * planes
    lane = lax.broadcasted_iota(I32, (size, 128), 1)
    sub = lax.broadcasted_iota(I32, (size, 128), 0)

    def activity(index):
        plane, term = index % planes, index // planes
        order = jnp.zeros_like(index)
        for i in range(kernels):
            order = jnp.where(plane == i, order_ref[i], order)
        degree = jnp.zeros_like(index)
        for t, powers in enumerate(TERMS):
            degree = jnp.where(term == t, powers[0] + powers[1], degree)
        wanted = (plane == kernels) | ((plane < kernels) & (degree <= order))
        return jnp.where(wanted & (index < size), 1.0, 0.0)

    active_row = activity(lane[:8])
    active_row = jnp.concatenate([active_row] * (size // 8), axis=0)
    active_col = activity(sub)
    lane16 = lane[:planes]
    row8 = lax.broadcasted_iota(I32, (8, 128), 0)
    for q in range(share):
        moments = parts[0][q]
        for ref in parts[1:]:
            moments = moments + ref[q]
        rows = []
        for a in range(terms):
            row = jnp.zeros((planes, 128), F32)
            for b in range(terms):
                left, right = block_of(a, b)
                at = right % LEFT * planes
                place = right // LEFT * LEFT + left
                piece = moments[at : at + planes]
                if b != place:
                    piece = pltpu.roll(piece, ((b - place) * planes) % 128, 1)
                row = jnp.where(lane16 // planes == b, piece, row)
            rows.append(row)
        paired = jnp.concatenate(rows, axis=0)
        target = pltpu.roll(paired, size - (planes - 1), 1)
        masked = active_row * active_col * paired
        system = jnp.where(lane == sub, masked + (1.0 + RIDGE * masked), masked)
        system = jnp.where(lane == size, active_col * target, system)
        blocks = [system[8 * m : 8 * m + 8] for m in range(size // 8)]
        for at in range(size // 8):
            wanted = [i for i in range(8) if (8 * at + i) % planes <= kernels]
            columns = [
                {i: jnp.broadcast_to(block[:, 8 * at + i : 8 * at + i + 1], (8, 128)) for i in wanted}
                for block in blocks
            ]
            inner, here = columns[at], blocks[at]
            for i in wanted:
                scale = 1.0 / jnp.broadcast_to(inner[i][i : i + 1], (8, 128))
                line = jnp.broadcast_to(here[i : i + 1], (8, 128)) * scale
                here = jnp.where(row8 == i, line, here - inner[i] * line)
                for k in wanted:
                    if k > i:
                        entry = jnp.broadcast_to(inner[k][i : i + 1], (8, 128)) * scale
                        inner[k] = jnp.where(row8 == i, entry, inner[k] - inner[i] * entry)
            lines = {i: jnp.broadcast_to(here[i : i + 1], (8, 128)) for i in wanted}
            for m in range(size // 8):
                if m == at:
                    blocks[m] = here
                    continue
                terms_here = [columns[m][i] * lines[i] for i in wanted]
                while len(terms_here) > 1:
                    terms_here = [
                        functools.reduce(lambda a, b: a + b, terms_here[q : q + 2])
                        for q in range(0, len(terms_here), 2)
                    ]
                blocks[m] = blocks[m] - terms_here[0]
        answer = jnp.concatenate(blocks, axis=0)
        answer = jnp.broadcast_to(answer[:, size : size + 1], (size, 128))
        answer = jnp.where(sub % planes == lane % planes, answer, 0.0)
        lines = [
            jnp.sum(answer[t * planes : (t + 1) * planes], axis=0, keepdims=True)
            for t in range(terms)
        ]
        lines.append(jnp.zeros((8 - terms, 128), F32))
        out[q] = jnp.concatenate(lines, axis=0)


def solve(order, parts, kernels, planes):
    share = parts[0].shape[0]
    return pl.pallas_call(
        functools.partial(solve_kernel, kernels=kernels, planes=planes, share=share),
        out_shape=jax.ShapeDtypeStruct((share, 8, 128), F32),
        in_specs=[SMEM] + [VMEM] * len(parts),
        out_specs=VMEM,
        compiler_params=params(4),
        name="solve",
    )(order, *parts)


def difference_kernel(
    me_ref,
    code_ref,
    row_ref,
    good_ref,
    *refs,
    calls,
    capacity,
    patches,
    ccds,
    share,
    kernels,
    planes,
    tall,
):
    coefs, stacks = refs[:ccds], refs[ccds : ccds + len(calls)]
    out, table, listing = refs[ccds + len(calls) :]
    strips, rows, columns = out.shape
    me, ccd, tiles = me_ref[0], me_ref[1], me_ref[2]
    for e in range(ccds):
        owner = ccd + e
        owner = jnp.where(owner >= ccds, owner - ccds, owner)
        for k in range(share):
            table[k * ccds + owner] = coefs[e][k]
    across = jnp.concatenate([across_rows(columns)] * (tall // 8), axis=0)
    across2 = across * across
    width = tall * planes
    lane = lax.broadcasted_iota(I32, (tall, width), 1)
    diagonal = lane // planes == lax.broadcasted_iota(I32, (tall, width), 0)
    is_science = diagonal & (lane % planes == planes - 1)
    sub = lax.broadcasted_iota(I32, (tall, columns), 0)

    def pieces(value):
        high = value.astype(BF16)
        rest = value - high.astype(F32)
        return high, rest.astype(BF16)

    for (first, groups), stack in zip(calls, stacks):

        def group(g, carry, first=first, stack=stack):
            patch = me + (first + g)
            patch = jnp.where(patch >= patches, patch - patches, patch)
            count = list_group(code_ref, listing, patch, tiles, strips)
            block = table[patch]
            coef = []
            for t in range(len(TERMS)):
                line = jnp.concatenate([block[t : t + 1]] * (width // 128), axis=1)
                coef.append(jnp.where(diagonal, -jnp.broadcast_to(line, (tall, width)), 0.0))
            coef[0] = jnp.where(is_science, 1.0, coef[0])
            twice = pieces(coef[2])

            def strip_step(t, carry):
                for j in range(PAIR):
                    j = jnp.minimum(t * PAIR + j, count - 1)
                    strip = listing[j]
                    offset, good = row_ref[strip], good_ref[strip]
                    for h in range(rows // tall):
                        v = (2 * (offset + h * tall + sub) + 1).astype(F32) / PATCH_ROWS - 1.0
                        v = jnp.concatenate([v] * (width // 128), axis=1)
                        plain = coef[0] + v * (coef[3] + v * coef[1])
                        once = coef[4] + v * coef[5]
                        lhs = jnp.concatenate([*pieces(plain), *pieces(once), *twice], axis=0)
                        rhs = stack[g * capacity + j, h * width : (h + 1) * width, :]
                        got = jnp.dot(lhs, rhs, preferred_element_type=F32)
                        part = [got[i * tall : (i + 1) * tall] for i in range(6)]
                        value = (
                            (part[0] + part[1])
                            + across * (part[2] + part[3])
                            + across2 * (part[4] + part[5])
                        )
                        value = jnp.where(h * tall + sub < good, value, 0.0)
                        out[strip, h * tall : (h + 1) * tall, :] = value.astype(BF16)
                return carry

            lax.fori_loop(0, (count + PAIR - 1) // PAIR, strip_step, 0)
            return carry

        if groups == 1:
            group(0, 0)
        else:
            lax.fori_loop(0, groups, group, 0)


def difference(scalars, coefs, stacks, calls, shape, sizes):
    capacity, patches, ccds, share, kernels, planes = sizes
    strips, rows, columns = shape
    return pl.pallas_call(
        functools.partial(
            difference_kernel,
            calls=calls,
            capacity=capacity,
            patches=patches,
            ccds=ccds,
            share=share,
            kernels=kernels,
            planes=planes,
            tall=16,
        ),
        out_shape=jax.ShapeDtypeStruct(shape, BF16),
        in_specs=[SMEM] * 4 + [VMEM] * (len(coefs) + len(stacks)),
        out_specs=VMEM,
        scratch_shapes=[
            pltpu.VMEM((share * ccds, 8, 128), F32),
            pltpu.SMEM((strips,), I32),
        ],
        compiler_params=params(20),
        name="difference",
    )(*scalars, *coefs, *stacks)


def shifted(value, axis, shift):
    size = lax.axis_size(axis)
    return lax.ppermute(value, axis, [(i, (i + shift) % size) for i in range(size)])


def body(
    science,
    strip_patch,
    strip_tile,
    strip_row,
    row_count,
    template,
    basis_rows,
    basis_cols,
    basis_order,
):
    patches, ccds = lax.axis_size("patch"), lax.axis_size("ccd")
    strips, rows, columns = science.shape
    tiles, tile_rows = template.shape[:2]
    kernels = basis_rows.shape[0]
    planes = -(-(kernels + 2) // 16) * 16
    capacity = max(2, 2 * strips // patches)
    share = -(-patches // ccds)
    sizes = (capacity, patches, ccds, share, kernels, planes)
    me = jnp.stack(
        [lax.axis_index("patch"), lax.axis_index("ccd"), jnp.int32(tiles)]
    ).astype(I32)
    code = strip_patch * tiles + strip_tile
    scalars = (me, code, strip_row, row_count)
    if patches <= 8:
        codes = [shifted(code, "patch", d) for d in range(1, patches)]
    else:
        everyone = lax.all_gather(code, "patch")
        mine = lax.axis_index("patch")
        codes = [
            lax.dynamic_index_in_dim(
                everyone, lax.rem(mine - d + patches, patches), 0, keepdims=False
            )
            for d in range(1, patches)
        ]
    tables = make_tables(basis_rows, basis_cols, rows, tile_rows, columns)
    chosen = select_tiles(me, codes, template, capacity)
    arrived = [shifted(tile, "patch", patches - d) for d, tile in enumerate(chosen, 1)]
    if patches <= 8:
        calls = [(d, 1) for d in range(patches)]
        plates = [template] + arrived
    else:
        calls = [(0, 1), (1, patches - 1)]
        plates = [template, jnp.concatenate(arrived, axis=0)]
    stacks, sums = [], []
    for (first, groups), plate in zip(calls, plates):
        last = first + groups == patches
        got = moments_call(
            scalars, plate, science, tables, sums if last else [], first, groups, first == 0, last,
            sizes,
        )
        stacks.append(got[0])
        if not last:
            sums.append(got[1])
        else:
            scattered = got[1:]
    mine = scattered[0]
    for e in range(1, ccds):
        mine = mine + shifted(scattered[e], "ccd", e)
    parts = [mine] + [shifted(mine, "patch", d) for d in range(1, patches)]
    coefficients = solve(basis_order, parts, kernels, planes)
    coefs = [coefficients] + [shifted(coefficients, "ccd", ccds - e) for e in range(1, ccds)]
    return difference(scalars, coefs, stacks, tuple(calls), science.shape, sizes)


def solution(mesh):
    spread = P(("groups", "patch", "ccd"))
    return jax.shard_map(
        body,
        mesh=mesh,
        in_specs=(spread,) * 6 + (P(), P(), P()),
        out_specs=spread,
        check_vma=False,
    )
```

```python
import functools

import jax
import jax.numpy as jnp
from jax import lax
from jax.experimental import pallas as pl
from jax.experimental.pallas import tpu as pltpu
from jax.sharding import PartitionSpec as P

PATCH_ROWS = 4000
RIDGE = 0.01
TERMS = ((0, 0), (2, 0), (0, 2), (1, 0), (0, 1), (1, 1))
LEFT = 3
BATCH = 4
PAIR = 2
VMEM = pl.BlockSpec(memory_space=pltpu.VMEM)
SMEM = pl.BlockSpec(memory_space=pltpu.SMEM)
CODE, ROW, GOOD, PATCH, ME, CCD = range(6)
OWN, REST, GROUP, START = range(4)
F32, BF16, I32 = jnp.float32, jnp.bfloat16, jnp.int32


def block_of(a, b):
    want = (TERMS[a][0] + TERMS[b][0], TERMS[a][1] + TERMS[b][1])
    for left in range(LEFT):
        for right in range(len(TERMS)):
            if (TERMS[left][0] + TERMS[right][0], TERMS[left][1] + TERMS[right][1]) == want:
                return left, right
    raise ValueError(want)


def params(mebibytes):
    return pltpu.CompilerParams(vmem_limit_bytes=mebibytes * 1024 * 1024)


def prepare_kernel(
    rows_ref,
    cols_ref,
    template,
    science,
    row_out,
    col_out,
    template_out,
    science_out,
    taps_held,
):
    kernels, taps = rows_ref.shape
    rows, columns = science.shape[1:]
    reach = template_out.shape[1]
    middle = taps // 2
    lag = (template.shape[1] - rows) // 2 - middle
    template_out[...] = template[:, lag : lag + reach, :]
    science_out[...] = science[...]
    taps_held[...] = jnp.zeros_like(taps_held)
    taps_held[0, :kernels, :taps] = rows_ref[...].astype(F32)
    taps_held[1, :kernels, :taps] = cols_ref[...].astype(F32)
    k = lax.broadcasted_iota(I32, (columns, columns), 0)
    lane = lax.broadcasted_iota(I32, (columns, columns), 1)
    moved_to = (k < taps) & ((k + lane == middle) | (k + lane == middle + columns))
    placed = jnp.dot(
        taps_held[1].astype(BF16),
        jnp.where(moved_to, 1.0, 0.0).astype(BF16),
        preferred_element_type=F32,
    )
    band = (k - lane <= middle) & (lane - k <= middle)
    for n in range(kernels):
        taps_n = jnp.broadcast_to(taps_held[0, n : n + 1, :], (rows, columns))
        moved = pltpu.roll(taps_n, 0, 1, stride=1, stride_axis=0)
        row_out[n * rows : (n + 1) * rows, :] = moved[:, :reach].astype(BF16)
        taps_n = jnp.broadcast_to(placed[n : n + 1, :], (columns, columns))
        moved = pltpu.roll(taps_n, 0, 1, stride=1, stride_axis=0)
        col_out[n] = jnp.where(band, moved, 0.0).astype(BF16)


def prepare(basis_rows, basis_cols, template, science):
    rows, columns = science.shape[1:]
    tiles, tile_rows = template.shape[:2]
    kernels, taps = basis_rows.shape
    reach = min(-(-(rows + taps - 1) // 8) * 8, (tile_rows + rows) // 2 + taps // 2)
    held_rows = -(-kernels // 16) * 16
    return pl.pallas_call(
        prepare_kernel,
        out_shape=(
            jax.ShapeDtypeStruct((kernels * rows, reach), BF16),
            jax.ShapeDtypeStruct((kernels, columns, columns), BF16),
            jax.ShapeDtypeStruct((tiles, reach, columns), BF16),
            jax.ShapeDtypeStruct(science.shape, BF16),
        ),
        in_specs=[VMEM] * 4,
        out_specs=[VMEM] * 4,
        scratch_shapes=[pltpu.VMEM((2, held_rows, columns), F32)],
        compiler_params=params(8),
        name="prepare",
    )(basis_rows, basis_cols, template, science)


def select_kernel(facts_ref, *refs, shifts, strips, tiles, capacity):
    others, template, outs = refs[:shifts], refs[shifts], refs[shifts + 1 : -1]
    listing = refs[-1]
    low = facts_ref[ME, 0] * tiles
    for other, out in zip(others, outs):
        for j in range(capacity):
            listing[j] = 0
        count = jnp.int32(0)
        for s in range(strips):
            tile = other[s] - low
            hit = (tile >= 0) & (tile < tiles)
            listing[count] = jnp.where(hit, tile, 0)
            count = count + hit.astype(I32)
        for j in range(capacity):
            out[j] = template[listing[j]]


def select_tiles(facts, others, template, capacity):
    shifts = len(others)
    strips = facts.shape[1]
    tiles, tile_rows, columns = template.shape
    return pl.pallas_call(
        functools.partial(
            select_kernel, shifts=shifts, strips=strips, tiles=tiles, capacity=capacity
        ),
        out_shape=[jax.ShapeDtypeStruct((capacity, tile_rows, columns), BF16)] * shifts,
        in_specs=[SMEM] * (1 + shifts) + [VMEM],
        out_specs=[VMEM] * shifts,
        scratch_shapes=[pltpu.SMEM((strips + capacity,), I32)],
        compiler_params=params(8),
        name="select",
    )(facts, *others, template)


def across_rows(columns):
    c = lax.broadcasted_iota(I32, (8, columns), 1)
    return (2 * c + 1).astype(F32) / columns - 1.0


def place(facts_ref, patch, patches):
    d = patch - facts_ref[ME, 0]
    return jnp.where(d < 0, d + patches, d)


def patch_at(facts_ref, e, k, ccds, patches):
    owner = facts_ref[CCD, 0] + e
    owner = jnp.where(owner >= ccds, owner - ccds, owner)
    return jnp.minimum(k * ccds + owner, patches - 1)


def write_lists(facts_ref, lists, patches, strips):
    me = facts_ref[ME, 0]
    groups = []
    for s in range(strips):
        d = facts_ref[PATCH, s] - me
        groups.append(jnp.where(d < 0, d + patches, d))

    def gather(d, row, count):
        for s in range(strips):
            lists[row, count] = s
            if row == REST:
                lists[GROUP, count] = d
            count = count + (groups[s] == d).astype(I32)
        return count

    def step(d, count):
        lists[START, d] = count
        return gather(d, REST, count)

    last = lists.shape[1] - 1
    lists[OWN, last] = gather(0, OWN, jnp.int32(0))
    lists[REST, last] = lax.fori_loop(1, patches, step, jnp.int32(0))


def moments_kernel(facts_ref, *refs, own, sizes):
    capacity, patches, ccds, share, tiles, kernels, planes = sizes
    if own:
        science, row_table, col_table, plates, lists, planes_out, sums, p32, running = refs
    else:
        lists, science, row_table, col_table, before, *arrived = refs[: -4 - ccds]
        planes_out, outs = refs[-4 - ccds], refs[-3 - ccds : -3]
        p32, running, plates = refs[-3:]
    strips, rows, columns = science.shape
    span = rows * planes
    unknowns = len(TERMS) * planes
    if kernels + 2 < planes:
        p32[...] = jnp.zeros_like(p32)
    across = jnp.concatenate([across_rows(columns)] * (planes // 8), axis=0)
    across = across.astype(BF16)
    step_rows = 8

    def gram(first_b, chosen, slots):
        offsets = [facts_ref[ROW, strip] for strip in chosen]
        totals = [jnp.zeros((unknowns, LEFT * planes), F32) for _ in chosen]
        row_iota = lax.broadcasted_iota(I32, (rows, columns), 0)
        heights = [
            (2 * (offset + row_iota) + 1).astype(F32) / PATCH_ROWS - 1.0 for offset in offsets
        ]
        for chunk in range(rows // step_rows):
            operands = []
            for i in range(len(chosen)):
                pieces = [[] for _ in TERMS]
                for r in range(chunk * step_rows, (chunk + 1) * step_rows):
                    at = r * planes
                    base = (first_b + i) * span + at
                    value = p32[base : base + planes, :].astype(BF16)
                    planes_out[slots[i], at : at + planes, :] = value
                    v = jnp.concatenate([jnp.broadcast_to(heights[i][r : r + 1], (8, columns))] * (planes // 8), axis=0)
                    with_v = value.astype(F32) * v
                    with_u = value * across
                    once = with_v.astype(BF16)
                    pieces[0].append(value)
                    pieces[1].append((with_v * v).astype(BF16))
                    pieces[2].append(with_u * across)
                    pieces[3].append(once)
                    pieces[4].append(with_u)
                    pieces[5].append(once * across)
                wide = [jnp.concatenate(part, axis=1) for part in pieces]
                operands.append(
                    (jnp.concatenate(wide, axis=0), jnp.concatenate(wide[:LEFT], axis=0))
                )
            for i, (every, left) in enumerate(operands):
                totals[i] = totals[i] + lax.dot_general(
                    every, left, (((1,), (1,)), ((), ())), preferred_element_type=F32
                )
        return totals

    if own:
        write_lists(facts_ref, lists, patches, strips)
    else:
        for d in range(1, patches):
            start = lists[START, d]
            source, base = (arrived[0], (d - 1) * capacity) if len(arrived) == 1 else (arrived[d - 1], 0)
            for i in range(capacity):
                plates[start + i] = source[base + i]
    row = OWN if own else REST
    count = lists[row, lists.shape[1] - 1]
    half = LEFT * planes
    running[...] = jnp.zeros_like(running)

    def batch(t, carry):
        slots = [t * BATCH + b for b in range(BATCH)]
        at = [jnp.minimum(slot, count - 1) for slot in slots]
        chosen = [lists[row, x] for x in at]
        if own:
            low = facts_ref[ME, 0] * tiles
            groups = [0] * BATCH
            stack = [plates[facts_ref[CODE, s] - low] for s in chosen]
        else:
            groups = [lists[GROUP, x] for x in at]
            stack = [plates[x] for x in at]
        smoothed = jnp.dot(
            row_table[...], jnp.concatenate(stack, axis=1), preferred_element_type=F32
        ).astype(BF16)
        usable = [
            jnp.where(
                lax.broadcasted_iota(I32, (rows, columns), 0)
                < jnp.where(slot < count, facts_ref[GOOD, strip], 0),
                1.0,
                0.0,
            )
            for slot, strip in zip(slots, chosen)
        ]
        for n in range(kernels):
            part = smoothed[n * rows : (n + 1) * rows]
            lhs = jnp.concatenate(
                [part[:, b * columns : (b + 1) * columns] for b in range(BATCH)], axis=0
            )
            convolved = jnp.dot(lhs, col_table[n], preferred_element_type=F32)
            for b in range(BATCH):
                p32[pl.ds(b * span + n, rows, stride=planes), :] = (
                    convolved[b * rows : (b + 1) * rows] * usable[b]
                )
        for b in range(BATCH):
            p32[pl.ds(b * span + kernels, rows, stride=planes), :] = usable[b]
            p32[pl.ds(b * span + planes - 1, rows, stride=planes), :] = (
                science[chosen[b]].astype(F32) * usable[b]
            )
        for b in range(0, BATCH, PAIR):

            @pl.when(slots[b] < count)
            def _(b=b):
                totals = gram(b, chosen[b : b + PAIR], slots[b : b + PAIR])
                for d, total in zip(groups[b : b + PAIR], totals):
                    running[d, :, :half] += total

        return carry

    lax.fori_loop(0, (count + BATCH - 1) // BATCH, batch, 0)

    def packed(total):
        return total[:half] + pltpu.roll(total[half:], half, 1)

    if own:
        sums[...] = packed(running[0])
        return
    running[0, :half] = before[...]
    for d in range(1, patches):
        running[d, :half] = packed(running[d])
    for e in range(ccds):
        for k in range(share):
            d = place(facts_ref, patch_at(facts_ref, e, k, ccds, patches), patches)
            outs[e][k] = running[d, :half]


def moments_call(facts, lists, science, tables, before, plates, sizes):
    capacity, patches, ccds, share, tiles, kernels, planes = sizes
    strips, rows, columns = science.shape
    own = before is None
    held = -(-strips // BATCH) * BATCH
    one_sum = (LEFT * planes, 128)
    scratch = [
        pltpu.VMEM((BATCH * rows * planes, columns), F32),
        pltpu.VMEM((1 if own else patches, len(TERMS) * planes, 128), F32),
    ]
    if own:
        held = min(held, -(-capacity // BATCH) * BATCH)
        arguments = [facts, science, *tables, *plates]
        outs = [jax.ShapeDtypeStruct((4, max(strips, patches) + 2), I32)]
        sums = [jax.ShapeDtypeStruct(one_sum, F32)]
    else:
        arguments = [facts, lists, science, *tables, before, *plates]
        outs = []
        sums = [jax.ShapeDtypeStruct((share,) + one_sum, F32)] * ccds
        scratch.append(pltpu.VMEM((strips + capacity,) + plates[0].shape[1:], BF16))
    scalars = 1 if own else 2
    return pl.pallas_call(
        functools.partial(moments_kernel, own=own, sizes=sizes),
        out_shape=outs + [jax.ShapeDtypeStruct((held, rows * planes, columns), BF16)] + sums,
        in_specs=[SMEM] * scalars + [VMEM] * (len(arguments) - scalars),
        out_specs=[SMEM] * len(outs) + [VMEM] * (1 + len(sums)),
        scratch_shapes=scratch,
        compiler_params=params(20),
        cost_estimate=pl.CostEstimate(flops=1 << 20, bytes_accessed=1 << 10, transcendentals=0),
        name="moments",
    )(*arguments)


def solve_kernel(order_ref, *refs, kernels, planes):
    parts, out = refs[:-1], refs[-1]
    terms = len(TERMS)
    size = terms * planes
    lane = lax.broadcasted_iota(I32, (size, 128), 1)
    sub = lax.broadcasted_iota(I32, (size, 128), 0)

    def activity(index):
        plane, term = index % planes, index // planes
        order = jnp.zeros_like(index)
        for i in range(kernels):
            order = jnp.where(plane == i, order_ref[i], order)
        degree = jnp.zeros_like(index)
        for t, powers in enumerate(TERMS):
            degree = jnp.where(term == t, powers[0] + powers[1], degree)
        wanted = (plane == kernels) | ((plane < kernels) & (degree <= order))
        return jnp.where(wanted & (index < size), 1.0, 0.0)

    active_row = activity(lane[:8])
    active_row = jnp.concatenate([active_row] * (size // 8), axis=0)
    active_col = activity(sub)
    lane16 = lane[:planes]
    row8 = lax.broadcasted_iota(I32, (8, 128), 0)
    for q in range(out.shape[0]):
        moments = parts[0][q]
        for ref in parts[1:]:
            moments = moments + ref[q]
        rows = []
        for a in range(terms):
            row = jnp.zeros((planes, 128), F32)
            for b in range(terms):
                left, right = block_of(a, b)
                at = right % LEFT * planes
                place = right // LEFT * LEFT + left
                piece = moments[at : at + planes]
                if b != place:
                    piece = pltpu.roll(piece, ((b - place) * planes) % 128, 1)
                row = jnp.where(lane16 // planes == b, piece, row)
            rows.append(row)
        paired = jnp.concatenate(rows, axis=0)
        target = pltpu.roll(paired, size - (planes - 1), 1)
        masked = active_row * active_col * paired
        system = jnp.where(lane == sub, masked + (1.0 + RIDGE * masked), masked)
        system = jnp.where(lane == size, active_col * target, system)
        blocks = [system[8 * m : 8 * m + 8] for m in range(size // 8)]
        for at in range(size // 8):
            wanted = [i for i in range(8) if (8 * at + i) % planes <= kernels]
            columns = [
                {i: jnp.broadcast_to(block[:, 8 * at + i : 8 * at + i + 1], (8, 128)) for i in wanted}
                for block in blocks
            ]
            inner, here = columns[at], blocks[at]
            for i in wanted:
                scale = 1.0 / jnp.broadcast_to(inner[i][i : i + 1], (8, 128))
                line = jnp.broadcast_to(here[i : i + 1], (8, 128)) * scale
                here = jnp.where(row8 == i, line, here - inner[i] * line)
                for k in wanted:
                    if k > i:
                        entry = jnp.broadcast_to(inner[k][i : i + 1], (8, 128)) * scale
                        inner[k] = jnp.where(row8 == i, entry, inner[k] - inner[i] * entry)
            lines = {i: jnp.broadcast_to(here[i : i + 1], (8, 128)) for i in wanted}
            for m in range(size // 8):
                if m == at:
                    blocks[m] = here
                    continue
                terms_here = [columns[m][i] * lines[i] for i in wanted]
                while len(terms_here) > 1:
                    terms_here = [
                        functools.reduce(lambda a, b: a + b, terms_here[q : q + 2])
                        for q in range(0, len(terms_here), 2)
                    ]
                blocks[m] = blocks[m] - terms_here[0]
        answer = jnp.concatenate(blocks, axis=0)
        answer = jnp.broadcast_to(answer[:, size : size + 1], (size, 128))
        answer = jnp.where(sub % planes == lane % planes, answer, 0.0)
        lines = [
            jnp.sum(answer[t * planes : (t + 1) * planes], axis=0, keepdims=True)
            for t in range(terms)
        ]
        lines.append(jnp.zeros((8 - terms, 128), F32))
        out[q] = jnp.concatenate(lines, axis=0)


def solve(order, parts, kernels, planes):
    return pl.pallas_call(
        functools.partial(solve_kernel, kernels=kernels, planes=planes),
        out_shape=jax.ShapeDtypeStruct((parts[0].shape[0], 8, 128), F32),
        in_specs=[SMEM] + [VMEM] * len(parts),
        out_specs=VMEM,
        compiler_params=params(4),
        name="solve",
    )(order, *parts)


def difference_kernel(facts_ref, lists, *refs, sizes, tall):
    capacity, patches, ccds, share, tiles, kernels, planes = sizes
    coefs, stacks = refs[:ccds], refs[ccds : ccds + 2]
    out, table = refs[ccds + 2 :]
    strips, rows, columns = out.shape
    across = jnp.concatenate([across_rows(columns)] * (tall // 8), axis=0)
    across2 = across * across
    width = tall * planes
    lane = lax.broadcasted_iota(I32, (tall, width), 1)
    diagonal = lane // planes == lax.broadcasted_iota(I32, (tall, width), 0)
    is_science = diagonal & (lane % planes == planes - 1)
    sub = lax.broadcasted_iota(I32, (tall, columns), 0)

    def pieces(value):
        high = value.astype(BF16)
        rest = value - high.astype(F32)
        return high, rest.astype(BF16)

    for e in range(ccds):
        for k in range(share):
            d = place(facts_ref, patch_at(facts_ref, e, k, ccds, patches), patches)
            block = coefs[e][k]
            for t in range(len(TERMS)):
                line = jnp.concatenate([block[t : t + 1]] * (width // 128), axis=1)
                value = jnp.where(diagonal, -jnp.broadcast_to(line, (tall, width)), 0.0)
                table[d, t] = jnp.where(is_science, 1.0, value) if t == 0 else value

    for row, stack in zip((OWN, REST), stacks):
        count = lists[row, lists.shape[1] - 1]

        def step(t, carry, row=row, stack=stack, count=count):
            for i in range(PAIR):
                j = jnp.minimum(t * PAIR + i, count - 1)
                strip = lists[row, j]
                d = 0 if row == OWN else lists[GROUP, j]
                coef = [table[d, t] for t in range(len(TERMS))]
                twice = pieces(coef[2])
                offset, good = facts_ref[ROW, strip], facts_ref[GOOD, strip]
                for h in range(rows // tall):
                    v = (2 * (offset + h * tall + sub) + 1).astype(F32) / PATCH_ROWS - 1.0
                    v = jnp.concatenate([v] * (width // 128), axis=1)
                    plain = coef[0] + v * (coef[3] + v * coef[1])
                    once = coef[4] + v * coef[5]
                    lhs = jnp.concatenate([*pieces(plain), *pieces(once), *twice], axis=0)
                    rhs = stack[j, h * width : (h + 1) * width, :]
                    got = jnp.dot(lhs, rhs, preferred_element_type=F32)
                    part = [got[x * tall : (x + 1) * tall] for x in range(6)]
                    value = (
                        (part[0] + part[1])
                        + across * (part[2] + part[3])
                        + across2 * (part[4] + part[5])
                    )
                    value = jnp.where(h * tall + sub < good, value, 0.0)
                    out[strip, h * tall : (h + 1) * tall, :] = value.astype(BF16)
            return carry

        lax.fori_loop(0, (count + PAIR - 1) // PAIR, step, 0)


def difference(facts, lists, coefs, stacks, shape, sizes):
    patches, planes, tall = sizes[1], sizes[-1], 16
    return pl.pallas_call(
        functools.partial(difference_kernel, sizes=sizes, tall=tall),
        out_shape=jax.ShapeDtypeStruct(shape, BF16),
        in_specs=[SMEM] * 2 + [VMEM] * (len(coefs) + len(stacks)),
        out_specs=VMEM,
        scratch_shapes=[pltpu.VMEM((patches, len(TERMS), tall, tall * planes), F32)],
        compiler_params=params(20),
        name="difference",
    )(facts, lists, *coefs, *stacks)


def shifted(value, axis, shift):
    size = lax.axis_size(axis)
    return lax.ppermute(value, axis, [(i, (i + shift) % size) for i in range(size)])


def body(
    science,
    strip_patch,
    strip_tile,
    strip_row,
    row_count,
    template,
    basis_rows,
    basis_cols,
    basis_order,
):
    patches, ccds = lax.axis_size("patch"), lax.axis_size("ccd")
    strips = science.shape[0]
    tiles = template.shape[0]
    kernels = basis_rows.shape[0]
    planes = -(-(kernels + 2) // 16) * 16
    capacity = max(2, 2 * strips // patches)
    share = -(-patches // ccds)
    sizes = (capacity, patches, ccds, share, tiles, kernels, planes)
    code = strip_patch * tiles + strip_tile
    others = [shifted(code, "patch", d) for d in range(1, patches)]
    facts = jnp.stack(
        [code, strip_row, row_count, strip_patch]
        + [jnp.full_like(code, lax.axis_index(axis)) for axis in ("patch", "ccd")]
    )
    *tables, template, science = prepare(basis_rows, basis_cols, template, science)
    chosen = select_tiles(facts, others, template, capacity)
    plates = [shifted(tile, "patch", patches - d) for d, tile in enumerate(chosen, 1)]
    if patches > 8:
        plates = [jnp.concatenate(plates, axis=0)]
    lists, own_planes, before = moments_call(facts, None, science, tables, None, [template], sizes)
    planes_left, *scattered = moments_call(facts, lists, science, tables, before, plates, sizes)
    mine = scattered[0]
    for e in range(1, ccds):
        mine = mine + shifted(scattered[e], "ccd", e)
    parts = [mine] + [shifted(mine, "patch", d) for d in range(1, patches)]
    coefficients = solve(basis_order, parts, kernels, planes)
    coefs = [coefficients] + [shifted(coefficients, "ccd", ccds - e) for e in range(1, ccds)]
    return difference(facts, lists, coefs, [own_planes, planes_left], science.shape, sizes)


def solution(mesh):
    spread = P(("groups", "patch", "ccd"))
    return jax.shard_map(
        body,
        mesh=mesh,
        in_specs=(spread,) * 6 + (P(), P(), P()),
        out_specs=spread,
        check_vma=False,
    )
```

```python
import functools

import jax
import jax.numpy as jnp
from jax import lax
from jax.experimental import pallas as pl
from jax.experimental.pallas import tpu as pltpu
from jax.sharding import PartitionSpec as P

PATCH_ROWS = 4000
RIDGE = 0.01
TERMS = ((0, 0), (2, 0), (0, 2), (1, 0), (0, 1), (1, 1))
LEFT = 3
BATCH = 4
PAIR = 2
FOUR = 4
VMEM = pl.BlockSpec(memory_space=pltpu.VMEM)
SMEM = pl.BlockSpec(memory_space=pltpu.SMEM)
CODE, ROW, GOOD, PATCH, ME, CCD = range(6)
OWN, REST, GROUP, START = range(4)
F32, BF16, I32 = jnp.float32, jnp.bfloat16, jnp.int32


def block_of(a, b):
    want = (TERMS[a][0] + TERMS[b][0], TERMS[a][1] + TERMS[b][1])
    for left in range(LEFT):
        for right in range(len(TERMS)):
            if (TERMS[left][0] + TERMS[right][0], TERMS[left][1] + TERMS[right][1]) == want:
                return left, right
    raise ValueError(want)


def params(mebibytes):
    return pltpu.CompilerParams(vmem_limit_bytes=mebibytes * 1024 * 1024)


def prepare_kernel(
    taps_ref,
    template,
    row_out,
    col_out,
    template_out,
    taps_held,
):
    kernels, taps = taps_ref.shape[1:]
    rows, columns = row_out.shape[0] // kernels, template.shape[2]
    reach = template_out.shape[1]
    middle = taps // 2
    lag = (template.shape[1] - rows) // 2 - middle
    template_out[...] = template[:, lag : lag + reach, :]
    taps_held[...] = jnp.zeros_like(taps_held)
    taps_held[:, :kernels, :taps] = taps_ref[...]
    k = lax.broadcasted_iota(I32, (columns, columns), 0)
    lane = lax.broadcasted_iota(I32, (columns, columns), 1)
    moved_to = (k < taps) & ((k + lane == middle) | (k + lane == middle + columns))
    placed = jnp.dot(
        taps_held[1].astype(BF16),
        jnp.where(moved_to, 1.0, 0.0).astype(BF16),
        preferred_element_type=F32,
    )
    band = (k - lane <= middle) & (lane - k <= middle)
    for n in range(kernels):
        taps_n = jnp.broadcast_to(taps_held[0, n : n + 1, :], (rows, columns))
        moved = pltpu.roll(taps_n, 0, 1, stride=1, stride_axis=0)
        row_out[n * rows : (n + 1) * rows, :] = moved[:, :reach].astype(BF16)
        taps_n = jnp.broadcast_to(placed[n : n + 1, :], (columns, columns))
        moved = pltpu.roll(taps_n, 0, 1, stride=1, stride_axis=0)
        col_out[n] = jnp.where(band, moved, 0.0).astype(BF16)


def prepare(basis_rows, basis_cols, template, rows):
    tiles, tile_rows, columns = template.shape
    kernels, taps = basis_rows.shape
    reach = min(-(-(rows + taps - 1) // 8) * 8, (tile_rows + rows) // 2 + taps // 2)
    held_rows = -(-kernels // 16) * 16
    return pl.pallas_call(
        prepare_kernel,
        out_shape=(
            jax.ShapeDtypeStruct((kernels * rows, reach), BF16),
            jax.ShapeDtypeStruct((kernels, columns, columns), BF16),
            jax.ShapeDtypeStruct((tiles, reach, columns), BF16),
        ),
        in_specs=[VMEM] * 2,
        out_specs=[VMEM] * 3,
        scratch_shapes=[pltpu.VMEM((2, held_rows, columns), F32)],
        compiler_params=params(8),
        name="prepare",
    )(jnp.stack([basis_rows, basis_cols]).astype(F32), template)


def select_kernel(*refs, shifts, strips, tiles, capacity):
    others, template, outs = refs[:shifts], refs[shifts], refs[shifts + 1 : -1]
    listing = refs[-1]
    for other, out in zip(others, outs):
        for j in range(capacity):
            listing[j] = 0
        count = jnp.int32(0)
        for s in range(strips):
            tile = other[s]
            hit = (tile >= 0) & (tile < tiles)
            listing[count] = jnp.where(hit, tile, 0)
            count = count + hit.astype(I32)
        for j in range(capacity):
            out[j] = template[listing[j]]


def select_tiles(others, template, capacity):
    shifts = len(others)
    strips = others[0].shape[0]
    tiles, tile_rows, columns = template.shape
    return pl.pallas_call(
        functools.partial(
            select_kernel, shifts=shifts, strips=strips, tiles=tiles, capacity=capacity
        ),
        out_shape=[jax.ShapeDtypeStruct((capacity, tile_rows, columns), BF16)] * shifts,
        in_specs=[SMEM] * shifts + [VMEM],
        out_specs=[VMEM] * shifts,
        scratch_shapes=[pltpu.SMEM((strips + capacity,), I32)],
        compiler_params=params(8),
        name="select",
    )(*others, template)


def across_rows(columns):
    c = lax.broadcasted_iota(I32, (8, columns), 1)
    return (2 * c + 1).astype(F32) / columns - 1.0


def place(facts_ref, patch, patches):
    d = patch - facts_ref[ME, 0]
    return jnp.where(d < 0, d + patches, d)


def patch_at(facts_ref, e, k, ccds, patches):
    owner = facts_ref[CCD, 0] + e
    owner = jnp.where(owner >= ccds, owner - ccds, owner)
    return jnp.minimum(k * ccds + owner, patches - 1)


def write_lists(facts_ref, lists, patches, strips):
    me = facts_ref[ME, 0]
    groups = []
    for s in range(strips):
        d = facts_ref[PATCH, s] - me
        groups.append(jnp.where(d < 0, d + patches, d))

    def gather(d, row, count):
        for s in range(strips):
            lists[row, count] = s
            if row == REST:
                lists[GROUP, count] = d
            count = count + (groups[s] == d).astype(I32)
        return count

    def step(d, count):
        lists[START, d] = count
        return gather(d, REST, count)

    last = lists.shape[1] - 1
    lists[OWN, last] = gather(0, OWN, jnp.int32(0))
    lists[REST, last] = lax.fori_loop(1, patches, step, jnp.int32(0))


def moments_kernel(facts_ref, *refs, own, sizes):
    capacity, patches, ccds, share, tiles, kernels, planes = sizes
    if own:
        science, row_table, col_table, plates, lists, science_out, planes_out, sums, p32, running = refs
    else:
        lists, science, row_table, col_table, before, *arrived = refs[: -4 - ccds]
        planes_out, outs = refs[-4 - ccds], refs[-3 - ccds : -3]
        p32, running, plates = refs[-3:]
    strips, rows, columns = science.shape
    span = rows * planes
    unknowns = len(TERMS) * planes
    if kernels + 2 < planes:
        p32[...] = jnp.zeros_like(p32)
    across = jnp.concatenate([across_rows(columns)] * (planes // 8), axis=0)
    across = across.astype(BF16)
    step_rows = 8

    def gram(first_b, chosen, slots):
        offsets = [facts_ref[ROW, strip] for strip in chosen]
        totals = [jnp.zeros((unknowns, LEFT * planes), F32) for _ in chosen]
        row_iota = lax.broadcasted_iota(I32, (rows, columns), 0)
        heights = [
            (2 * (offset + row_iota) + 1).astype(F32) / PATCH_ROWS - 1.0 for offset in offsets
        ]
        for chunk in range(rows // step_rows):
            operands = []
            for i in range(len(chosen)):
                pieces = [[] for _ in TERMS]
                for r in range(chunk * step_rows, (chunk + 1) * step_rows):
                    at = r * planes
                    base = (first_b + i) * span + at
                    value = p32[base : base + planes, :].astype(BF16)
                    planes_out[slots[i], at : at + planes, :] = value
                    v = jnp.concatenate([jnp.broadcast_to(heights[i][r : r + 1], (8, columns))] * (planes // 8), axis=0)
                    with_v = value.astype(F32) * v
                    with_u = value * across
                    once = with_v.astype(BF16)
                    pieces[0].append(value)
                    pieces[1].append((with_v * v).astype(BF16))
                    pieces[2].append(with_u * across)
                    pieces[3].append(once)
                    pieces[4].append(with_u)
                    pieces[5].append(once * across)
                wide = [jnp.concatenate(part, axis=1) for part in pieces]
                operands.append(
                    (jnp.concatenate(wide, axis=0), jnp.concatenate(wide[:LEFT], axis=0))
                )
            for i, (every, left) in enumerate(operands):
                totals[i] = totals[i] + lax.dot_general(
                    every, left, (((1,), (1,)), ((), ())), preferred_element_type=F32
                )
        return totals

    if own:
        write_lists(facts_ref, lists, patches, strips)
        science_out[...] = science[...]
    else:
        for d in range(1, patches):
            start = lists[START, d]
            source, base = (arrived[0], (d - 1) * capacity) if len(arrived) == 1 else (arrived[d - 1], 0)
            for i in range(capacity):
                plates[start + i] = source[base + i]
    row = OWN if own else REST
    count = lists[row, lists.shape[1] - 1]
    half = LEFT * planes
    running[...] = jnp.zeros_like(running)

    def batch(t, carry):
        slots = [t * BATCH + b for b in range(BATCH)]
        at = [jnp.minimum(slot, count - 1) for slot in slots]
        chosen = [lists[row, x] for x in at]
        if own:
            low = facts_ref[ME, 0] * tiles
            groups = [0] * BATCH
            stack = [plates[facts_ref[CODE, s] - low] for s in chosen]
        else:
            groups = [lists[GROUP, x] for x in at]
            stack = [plates[x] for x in at]
        smoothed = jnp.dot(
            row_table[...], jnp.concatenate(stack, axis=1), preferred_element_type=F32
        ).astype(BF16)
        usable = [
            jnp.where(
                lax.broadcasted_iota(I32, (rows, columns), 0)
                < jnp.where(slot < count, facts_ref[GOOD, strip], 0),
                1.0,
                0.0,
            )
            for slot, strip in zip(slots, chosen)
        ]
        for n in range(kernels):
            part = smoothed[n * rows : (n + 1) * rows]
            lhs = jnp.concatenate(
                [part[:, b * columns : (b + 1) * columns] for b in range(BATCH)], axis=0
            )
            convolved = jnp.dot(lhs, col_table[n], preferred_element_type=F32)
            for b in range(BATCH):
                p32[pl.ds(b * span + n, rows, stride=planes), :] = (
                    convolved[b * rows : (b + 1) * rows] * usable[b]
                )
        for b in range(BATCH):
            p32[pl.ds(b * span + kernels, rows, stride=planes), :] = usable[b]
            p32[pl.ds(b * span + planes - 1, rows, stride=planes), :] = (
                science[chosen[b]].astype(F32) * usable[b]
            )
        for b in range(0, BATCH, PAIR):

            @pl.when(slots[b] < count)
            def _(b=b):
                totals = gram(b, chosen[b : b + PAIR], slots[b : b + PAIR])
                for d, total in zip(groups[b : b + PAIR], totals):
                    running[d, :, :half] += total

        return carry

    lax.fori_loop(0, (count + BATCH - 1) // BATCH, batch, 0)

    def packed(total):
        return total[:half] + pltpu.roll(total[half:], half, 1)

    if own:
        sums[...] = packed(running[0])
        return
    running[0, :half] = before[...]
    for d in range(1, patches):
        running[d, :half] = packed(running[d])
    for e in range(ccds):
        for k in range(share):
            d = place(facts_ref, patch_at(facts_ref, e, k, ccds, patches), patches)
            outs[e][k] = running[d, :half]


def moments_call(facts, lists, science, tables, before, plates, sizes):
    capacity, patches, ccds, share, tiles, kernels, planes = sizes
    strips, rows, columns = science.shape
    own = before is None
    held = -(-strips // BATCH) * BATCH
    one_sum = (LEFT * planes, 128)
    scratch = [
        pltpu.VMEM((BATCH * rows * planes, columns), F32),
        pltpu.VMEM((1 if own else patches, len(TERMS) * planes, 128), F32),
    ]
    if own:
        held = min(held, -(-capacity // BATCH) * BATCH)
        arguments = [facts, science, *tables, *plates]
        outs = [jax.ShapeDtypeStruct((4, max(strips, patches) + 2), I32)]
        passed = [jax.ShapeDtypeStruct(science.shape, BF16)]
        sums = [jax.ShapeDtypeStruct(one_sum, F32)]
    else:
        arguments = [facts, lists, science, *tables, before, *plates]
        outs, passed = [], []
        sums = [jax.ShapeDtypeStruct((share,) + one_sum, F32)] * ccds
        scratch.append(pltpu.VMEM((strips + capacity,) + plates[0].shape[1:], BF16))
    scalars = 1 if own else 2
    return pl.pallas_call(
        functools.partial(moments_kernel, own=own, sizes=sizes),
        out_shape=outs + passed + [jax.ShapeDtypeStruct((held, rows * planes, columns), BF16)] + sums,
        in_specs=[SMEM] * scalars + [VMEM] * (len(arguments) - scalars),
        out_specs=[SMEM] * len(outs) + [VMEM] * (len(passed) + 1 + len(sums)),
        scratch_shapes=scratch,
        compiler_params=params(20),
        cost_estimate=pl.CostEstimate(flops=1 << 20, bytes_accessed=1 << 10, transcendentals=0),
        name="moments",
    )(*arguments)


def solve_kernel(order_ref, *refs, kernels, planes):
    parts, out = refs[:-1], refs[-1]
    terms = len(TERMS)
    size = terms * planes
    lane = lax.broadcasted_iota(I32, (size, 128), 1)
    sub = lax.broadcasted_iota(I32, (size, 128), 0)

    def activity(index):
        plane, term = index % planes, index // planes
        order = jnp.zeros_like(index)
        for i in range(kernels):
            order = jnp.where(plane == i, order_ref[i], order)
        degree = jnp.zeros_like(index)
        for t, powers in enumerate(TERMS):
            degree = jnp.where(term == t, powers[0] + powers[1], degree)
        wanted = (plane == kernels) | ((plane < kernels) & (degree <= order))
        return jnp.where(wanted & (index < size), 1.0, 0.0)

    active_row = activity(lane[:8])
    active_row = jnp.concatenate([active_row] * (size // 8), axis=0)
    active_col = activity(sub)
    lane16 = lane[:planes]
    row8 = lax.broadcasted_iota(I32, (8, 128), 0)
    for q in range(out.shape[0]):
        moments = parts[0][q]
        for ref in parts[1:]:
            moments = moments + ref[q]
        rows = []
        for a in range(terms):
            row = jnp.zeros((planes, 128), F32)
            for b in range(terms):
                left, right = block_of(a, b)
                at = right % LEFT * planes
                place = right // LEFT * LEFT + left
                piece = moments[at : at + planes]
                if b != place:
                    piece = pltpu.roll(piece, ((b - place) * planes) % 128, 1)
                row = jnp.where(lane16 // planes == b, piece, row)
            rows.append(row)
        paired = jnp.concatenate(rows, axis=0)
        target = pltpu.roll(paired, size - (planes - 1), 1)
        masked = active_row * active_col * paired
        system = jnp.where(lane == sub, masked + (1.0 + RIDGE * masked), masked)
        system = jnp.where(lane == size, active_col * target, system)
        blocks = [system[8 * m : 8 * m + 8] for m in range(size // 8)]
        for at in range(size // 8):
            wanted = [i for i in range(8) if (8 * at + i) % planes <= kernels]
            columns = [
                {i: jnp.broadcast_to(block[:, 8 * at + i : 8 * at + i + 1], (8, 128)) for i in wanted}
                for block in blocks
            ]
            inner, here = columns[at], blocks[at]
            for i in wanted:
                pivot = jnp.broadcast_to(inner[i][i : i + 1], (8, 128))
                scale = pl.reciprocal(pivot, approx=True)
                scale = scale * (2.0 - pivot * scale)
                scale = scale * (2.0 - pivot * scale)
                line = jnp.broadcast_to(here[i : i + 1], (8, 128)) * scale
                here = jnp.where(row8 == i, line, here - inner[i] * line)
                for k in wanted:
                    if k > i:
                        entry = jnp.broadcast_to(inner[k][i : i + 1], (8, 128)) * scale
                        inner[k] = jnp.where(row8 == i, entry, inner[k] - inner[i] * entry)
            lines = {i: jnp.broadcast_to(here[i : i + 1], (8, 128)) for i in wanted}
            for m in range(size // 8):
                if m == at:
                    blocks[m] = here
                    continue
                terms_here = [columns[m][i] * lines[i] for i in wanted]
                while len(terms_here) > 1:
                    terms_here = [
                        functools.reduce(lambda a, b: a + b, terms_here[q : q + 2])
                        for q in range(0, len(terms_here), 2)
                    ]
                blocks[m] = blocks[m] - terms_here[0]
        answer = jnp.concatenate(blocks, axis=0)
        answer = jnp.broadcast_to(answer[:, size : size + 1], (size, 128))
        answer = jnp.where(sub % planes == lane % planes, answer, 0.0)
        lines = [
            jnp.sum(answer[t * planes : (t + 1) * planes], axis=0, keepdims=True)
            for t in range(terms)
        ]
        lines.append(jnp.zeros((8 - terms, 128), F32))
        out[q] = jnp.concatenate(lines, axis=0)


def solve(order, parts, kernels, planes):
    return pl.pallas_call(
        functools.partial(solve_kernel, kernels=kernels, planes=planes),
        out_shape=jax.ShapeDtypeStruct((parts[0].shape[0], 8, 128), F32),
        in_specs=[SMEM] + [VMEM] * len(parts),
        out_specs=VMEM,
        compiler_params=params(4),
        name="solve",
    )(order, *parts)


def difference_kernel(facts_ref, lists, *refs, sizes, tall):
    capacity, patches, ccds, share, tiles, kernels, planes = sizes
    coefs, stacks = refs[:ccds], refs[ccds : ccds + 2]
    out, table = refs[ccds + 2 :]
    strips, rows, columns = out.shape
    across = jnp.concatenate([across_rows(columns)] * (tall // 8), axis=0)
    across2 = across * across
    width = tall * planes
    lane = lax.broadcasted_iota(I32, (tall, width), 1)
    diagonal = lane // planes == lax.broadcasted_iota(I32, (tall, width), 0)
    is_science = diagonal & (lane % planes == planes - 1)
    sub = lax.broadcasted_iota(I32, (tall, columns), 0)

    def pieces(value):
        high = value.astype(BF16)
        rest = value - high.astype(F32)
        return high, rest.astype(BF16)

    for e in range(ccds):
        for k in range(share):
            d = place(facts_ref, patch_at(facts_ref, e, k, ccds, patches), patches)
            block = coefs[e][k]
            for t in range(len(TERMS)):
                line = jnp.concatenate([block[t : t + 1]] * (width // 128), axis=1)
                value = jnp.where(diagonal, -jnp.broadcast_to(line, (tall, width)), 0.0)
                table[d, t] = jnp.where(is_science, 1.0, value) if t == 0 else value

    for row, stack in zip((OWN, REST), stacks):
        count = lists[row, lists.shape[1] - 1]

        def step(t, carry, row=row, stack=stack, count=count):
            for i in range(FOUR):
                j = jnp.minimum(t * FOUR + i, count - 1)
                strip = lists[row, j]
                d = 0 if row == OWN else lists[GROUP, j]
                coef = [table[d, t] for t in range(len(TERMS))]
                twice = pieces(coef[2])
                offset, good = facts_ref[ROW, strip], facts_ref[GOOD, strip]
                for h in range(rows // tall):
                    v = (2 * (offset + h * tall + sub) + 1).astype(F32) / PATCH_ROWS - 1.0
                    v = jnp.concatenate([v] * (width // 128), axis=1)
                    plain = coef[0] + v * (coef[3] + v * coef[1])
                    once = coef[4] + v * coef[5]
                    lhs = jnp.concatenate([*pieces(plain), *pieces(once), *twice], axis=0)
                    rhs = stack[j, h * width : (h + 1) * width, :]
                    got = jnp.dot(lhs, rhs, preferred_element_type=F32)
                    part = [got[x * tall : (x + 1) * tall] for x in range(6)]
                    value = (
                        (part[0] + part[1])
                        + across * (part[2] + part[3])
                        + across2 * (part[4] + part[5])
                    )
                    value = jnp.where(h * tall + sub < good, value, 0.0)
                    out[strip, h * tall : (h + 1) * tall, :] = value.astype(BF16)
            return carry

        lax.fori_loop(0, (count + FOUR - 1) // FOUR, step, 0)


def difference(facts, lists, coefs, stacks, shape, sizes):
    patches, planes, tall = sizes[1], sizes[-1], 16
    return pl.pallas_call(
        functools.partial(difference_kernel, sizes=sizes, tall=tall),
        out_shape=jax.ShapeDtypeStruct(shape, BF16),
        in_specs=[SMEM] * 2 + [VMEM] * (len(coefs) + len(stacks)),
        out_specs=VMEM,
        scratch_shapes=[pltpu.VMEM((patches, len(TERMS), tall, tall * planes), F32)],
        compiler_params=params(20),
        name="difference",
    )(facts, lists, *coefs, *stacks)


def shifted(value, axis, shift):
    size = lax.axis_size(axis)
    return lax.ppermute(value, axis, [(i, (i + shift) % size) for i in range(size)])


def body(
    science,
    strip_patch,
    strip_tile,
    strip_row,
    row_count,
    template,
    basis_rows,
    basis_cols,
    basis_order,
):
    patches, ccds = lax.axis_size("patch"), lax.axis_size("ccd")
    strips = science.shape[0]
    tiles = template.shape[0]
    kernels = basis_rows.shape[0]
    planes = -(-(kernels + 2) // 16) * 16
    capacity = max(2, 2 * strips // patches)
    share = -(-patches // ccds)
    sizes = (capacity, patches, ccds, share, tiles, kernels, planes)
    code = strip_patch * tiles + strip_tile
    me = lax.axis_index("patch")
    others = []
    for d in range(1, patches):
        owner = jnp.where(me + d >= patches, me + d - patches, me + d)
        others.append(shifted(code - owner * tiles, "patch", d))
    facts = jnp.stack(
        [code, strip_row, row_count, strip_patch]
        + [jnp.full_like(code, lax.axis_index(axis)) for axis in ("patch", "ccd")]
    )
    *tables, template = prepare(basis_rows, basis_cols, template, science.shape[1])
    chosen = select_tiles(others, template, capacity)
    plates = [shifted(tile, "patch", patches - d) for d, tile in enumerate(chosen, 1)]
    if patches > 8:
        plates = [jnp.concatenate(plates, axis=0)]
    lists, science, own_planes, before = moments_call(facts, None, science, tables, None, [template], sizes)
    planes_left, *scattered = moments_call(facts, lists, science, tables, before, plates, sizes)
    mine = scattered[0]
    for e in range(1, ccds):
        mine = mine + shifted(scattered[e], "ccd", e)
    parts = [mine] + [shifted(mine, "patch", d) for d in range(1, patches)]
    coefficients = solve(basis_order, parts, kernels, planes)
    coefs = [coefficients] + [shifted(coefficients, "ccd", ccds - e) for e in range(1, ccds)]
    return difference(facts, lists, coefs, [own_planes, planes_left], science.shape, sizes)


def solution(mesh):
    spread = P(("groups", "patch", "ccd"))
    return jax.shard_map(
        body,
        mesh=mesh,
        in_specs=(spread,) * 6 + (P(), P(), P()),
        out_specs=spread,
        check_vma=False,
    )
```

```python
import functools

import jax
import jax.numpy as jnp
from jax import lax
from jax.experimental import pallas as pl
from jax.experimental.pallas import tpu as pltpu
from jax.sharding import PartitionSpec as P

PATCH_ROWS = 4000
RIDGE = 0.01
TERMS = ((0, 0), (2, 0), (0, 2), (1, 0), (0, 1), (1, 1))
LEFT = 3
BATCH = 4
PAIR = 2
FOUR = 4
VMEM = pl.BlockSpec(memory_space=pltpu.VMEM)
SMEM = pl.BlockSpec(memory_space=pltpu.SMEM)
CODE, ROW, GOOD, PATCH, ME, CCD = range(6)
OWN, REST, GROUP, START = range(4)
F32, BF16, I32 = jnp.float32, jnp.bfloat16, jnp.int32


def block_of(a, b):
    want = (TERMS[a][0] + TERMS[b][0], TERMS[a][1] + TERMS[b][1])
    for left in range(LEFT):
        for right in range(len(TERMS)):
            if (TERMS[left][0] + TERMS[right][0], TERMS[left][1] + TERMS[right][1]) == want:
                return left, right
    raise ValueError(want)


def params(mebibytes):
    return pltpu.CompilerParams(vmem_limit_bytes=mebibytes * 1024 * 1024)


def prepare_kernel(
    taps_ref,
    template,
    row_out,
    col_out,
    template_out,
    taps_held,
):
    kernels, taps = taps_ref.shape[1:]
    rows, columns = row_out.shape[0] // kernels, template.shape[2]
    reach = template_out.shape[1]
    middle = taps // 2
    lag = (template.shape[1] - rows) // 2 - middle
    template_out[...] = template[:, lag : lag + reach, :]
    taps_held[...] = jnp.zeros_like(taps_held)
    taps_held[:, :kernels, :taps] = taps_ref[...]
    k = lax.broadcasted_iota(I32, (columns, columns), 0)
    lane = lax.broadcasted_iota(I32, (columns, columns), 1)
    moved_to = (k < taps) & ((k + lane == middle) | (k + lane == middle + columns))
    placed = jnp.dot(
        taps_held[1].astype(BF16),
        jnp.where(moved_to, 1.0, 0.0).astype(BF16),
        preferred_element_type=F32,
    )
    band = (k - lane <= middle) & (lane - k <= middle)
    for n in range(kernels):
        taps_n = jnp.broadcast_to(taps_held[0, n : n + 1, :], (rows, columns))
        moved = pltpu.roll(taps_n, 0, 1, stride=1, stride_axis=0)
        row_out[n * rows : (n + 1) * rows, :] = moved[:, :reach].astype(BF16)
        taps_n = jnp.broadcast_to(placed[n : n + 1, :], (columns, columns))
        moved = pltpu.roll(taps_n, 0, 1, stride=1, stride_axis=0)
        col_out[n] = jnp.where(band, moved, 0.0).astype(BF16)


def prepare(basis_rows, basis_cols, template, rows):
    tiles, tile_rows, columns = template.shape
    kernels, taps = basis_rows.shape
    reach = min(-(-(rows + taps - 1) // 8) * 8, (tile_rows + rows) // 2 + taps // 2)
    held_rows = -(-kernels // 16) * 16
    return pl.pallas_call(
        prepare_kernel,
        out_shape=(
            jax.ShapeDtypeStruct((kernels * rows, reach), BF16),
            jax.ShapeDtypeStruct((kernels, columns, columns), BF16),
            jax.ShapeDtypeStruct((tiles, reach, columns), BF16),
        ),
        in_specs=[VMEM] * 2,
        out_specs=[VMEM] * 3,
        scratch_shapes=[pltpu.VMEM((2, held_rows, columns), F32)],
        compiler_params=params(8),
        name="prepare",
    )(jnp.stack([basis_rows, basis_cols]).astype(F32), template)


def select_kernel(*refs, shifts, strips, tiles, capacity):
    others, template, outs = refs[:shifts], refs[shifts], refs[shifts + 1 : -1]
    listing = refs[-1]
    for other, out in zip(others, outs):
        for j in range(capacity):
            listing[j] = 0
        count = jnp.int32(0)
        for s in range(strips):
            tile = other[s]
            hit = (tile >= 0) & (tile < tiles)
            listing[count] = jnp.where(hit, tile, 0)
            count = count + hit.astype(I32)
        for j in range(capacity):
            out[j] = template[listing[j]]


def select_tiles(others, template, capacity):
    shifts = len(others)
    strips = others[0].shape[0]
    tiles, tile_rows, columns = template.shape
    return pl.pallas_call(
        functools.partial(
            select_kernel, shifts=shifts, strips=strips, tiles=tiles, capacity=capacity
        ),
        out_shape=[jax.ShapeDtypeStruct((capacity, tile_rows, columns), BF16)] * shifts,
        in_specs=[SMEM] * shifts + [VMEM],
        out_specs=[VMEM] * shifts,
        scratch_shapes=[pltpu.SMEM((strips + capacity,), I32)],
        compiler_params=params(8),
        name="select",
    )(*others, template)


def across_rows(columns):
    c = lax.broadcasted_iota(I32, (8, columns), 1)
    return (2 * c + 1).astype(F32) / columns - 1.0


def place(facts_ref, patch, patches):
    d = patch - facts_ref[ME, 0]
    return jnp.where(d < 0, d + patches, d)


def patch_at(facts_ref, e, k, ccds, patches):
    owner = facts_ref[CCD, 0] + e
    owner = jnp.where(owner >= ccds, owner - ccds, owner)
    return jnp.minimum(k * ccds + owner, patches - 1)


def write_lists(facts_ref, lists, patches, strips):
    me = facts_ref[ME, 0]
    groups = []
    for s in range(strips):
        d = facts_ref[PATCH, s] - me
        groups.append(jnp.where(d < 0, d + patches, d))

    def gather(d, row, count):
        for s in range(strips):
            lists[row, count] = s
            if row == REST:
                lists[GROUP, count] = d
            count = count + (groups[s] == d).astype(I32)
        return count

    def step(d, count):
        lists[START, d] = count
        return gather(d, REST, count)

    last = lists.shape[1] - 1
    lists[OWN, last] = gather(0, OWN, jnp.int32(0))
    lists[REST, last] = lax.fori_loop(1, patches, step, jnp.int32(0))


def moments_kernel(facts_ref, *refs, own, sizes):
    capacity, patches, ccds, share, tiles, kernels, planes = sizes
    if own:
        science, row_table, col_table, plates, lists, science_out, planes_out, sums, p32, running = refs
    else:
        lists, science, row_table, col_table, before, *arrived = refs[: -4 - ccds]
        planes_out, outs = refs[-4 - ccds], refs[-3 - ccds : -3]
        p32, running, plates = refs[-3:]
    strips, rows, columns = science.shape
    span = rows * planes
    unknowns = len(TERMS) * planes
    if kernels + 2 < planes:
        p32[...] = jnp.zeros_like(p32)
    across = jnp.concatenate([across_rows(columns)] * (planes // 8), axis=0)
    across = across.astype(BF16)
    step_rows = 8

    def gram(first_b, chosen, slots):
        offsets = [facts_ref[ROW, strip] for strip in chosen]
        totals = [jnp.zeros((unknowns, LEFT * planes), F32) for _ in chosen]
        row_iota = lax.broadcasted_iota(I32, (rows, columns), 0)
        heights = [
            (2 * (offset + row_iota) + 1).astype(F32) / PATCH_ROWS - 1.0 for offset in offsets
        ]
        for chunk in range(rows // step_rows):
            operands = []
            for i in range(len(chosen)):
                pieces = [[] for _ in TERMS]
                for r in range(chunk * step_rows, (chunk + 1) * step_rows):
                    at = r * planes
                    base = (first_b + i) * span + at
                    value = p32[base : base + planes, :].astype(BF16)
                    planes_out[slots[i], at : at + planes, :] = value
                    v = jnp.concatenate([jnp.broadcast_to(heights[i][r : r + 1], (8, columns))] * (planes // 8), axis=0)
                    with_v = value.astype(F32) * v
                    with_u = value * across
                    once = with_v.astype(BF16)
                    pieces[0].append(value)
                    pieces[1].append((with_v * v).astype(BF16))
                    pieces[2].append(with_u * across)
                    pieces[3].append(once)
                    pieces[4].append(with_u)
                    pieces[5].append(once * across)
                wide = [jnp.concatenate(part, axis=1) for part in pieces]
                operands.append(
                    (jnp.concatenate(wide, axis=0), jnp.concatenate(wide[:LEFT], axis=0))
                )
            for i, (every, left) in enumerate(operands):
                totals[i] = totals[i] + lax.dot_general(
                    every, left, (((1,), (1,)), ((), ())), preferred_element_type=F32
                )
        return totals

    if own:
        write_lists(facts_ref, lists, patches, strips)
        science_out[...] = science[...]
    else:
        for d in range(1, patches):
            start = lists[START, d]
            source, base = (arrived[0], (d - 1) * capacity) if len(arrived) == 1 else (arrived[d - 1], 0)
            for i in range(capacity):
                plates[start + i] = source[base + i]
    row = OWN if own else REST
    count = lists[row, lists.shape[1] - 1]
    half = LEFT * planes
    running[...] = jnp.zeros_like(running)

    def batch(t, carry):
        slots = [t * BATCH + b for b in range(BATCH)]
        at = [jnp.minimum(slot, count - 1) for slot in slots]
        chosen = [lists[row, x] for x in at]
        if own:
            low = facts_ref[ME, 0] * tiles
            groups = [0] * BATCH
            stack = [plates[facts_ref[CODE, s] - low] for s in chosen]
        else:
            groups = [lists[GROUP, x] for x in at]
            stack = [plates[x] for x in at]
        smoothed = jnp.dot(
            row_table[...], jnp.concatenate(stack, axis=1), preferred_element_type=F32
        ).astype(BF16)
        usable = [
            jnp.where(
                lax.broadcasted_iota(I32, (rows, columns), 0)
                < jnp.where(slot < count, facts_ref[GOOD, strip], 0),
                1.0,
                0.0,
            )
            for slot, strip in zip(slots, chosen)
        ]
        for n in range(kernels):
            part = smoothed[n * rows : (n + 1) * rows]
            lhs = jnp.concatenate(
                [part[:, b * columns : (b + 1) * columns] for b in range(BATCH)], axis=0
            )
            convolved = jnp.dot(lhs, col_table[n], preferred_element_type=F32)
            for b in range(BATCH):
                p32[pl.ds(b * span + n, rows, stride=planes), :] = (
                    convolved[b * rows : (b + 1) * rows] * usable[b]
                )
        for b in range(BATCH):
            p32[pl.ds(b * span + kernels, rows, stride=planes), :] = usable[b]
            p32[pl.ds(b * span + planes - 1, rows, stride=planes), :] = (
                science[chosen[b]].astype(F32) * usable[b]
            )
        for b in range(0, BATCH, PAIR):

            @pl.when(slots[b] < count)
            def _(b=b):
                totals = gram(b, chosen[b : b + PAIR], slots[b : b + PAIR])
                for d, total in zip(groups[b : b + PAIR], totals):
                    running[d, :, :half] += total

        return carry

    lax.fori_loop(0, (count + BATCH - 1) // BATCH, batch, 0)

    def packed(total):
        return total[:half] + pltpu.roll(total[half:], half, 1)

    if own:
        sums[...] = packed(running[0])
        return
    running[0, :half] = before[...]
    for d in range(1, patches):
        running[d, :half] = packed(running[d])
    for e in range(ccds):
        for k in range(share):
            d = place(facts_ref, patch_at(facts_ref, e, k, ccds, patches), patches)
            outs[e][k] = running[d, :half]


def moments_call(facts, lists, science, tables, before, plates, sizes):
    capacity, patches, ccds, share, tiles, kernels, planes = sizes
    strips, rows, columns = science.shape
    own = before is None
    held = -(-strips // BATCH) * BATCH
    one_sum = (LEFT * planes, 128)
    scratch = [
        pltpu.VMEM((BATCH * rows * planes, columns), F32),
        pltpu.VMEM((1 if own else patches, len(TERMS) * planes, 128), F32),
    ]
    if own:
        held = min(held, -(-capacity // BATCH) * BATCH)
        arguments = [facts, science, *tables, *plates]
        outs = [jax.ShapeDtypeStruct((4, max(strips, patches) + 2), I32)]
        passed = [jax.ShapeDtypeStruct(science.shape, BF16)]
        sums = [jax.ShapeDtypeStruct(one_sum, F32)]
    else:
        arguments = [facts, lists, science, *tables, before, *plates]
        outs, passed = [], []
        sums = [jax.ShapeDtypeStruct((share,) + one_sum, F32)] * ccds
        scratch.append(pltpu.VMEM((strips + capacity,) + plates[0].shape[1:], BF16))
    scalars = 1 if own else 2
    return pl.pallas_call(
        functools.partial(moments_kernel, own=own, sizes=sizes),
        out_shape=outs + passed + [jax.ShapeDtypeStruct((held, rows * planes, columns), BF16)] + sums,
        in_specs=[SMEM] * scalars + [VMEM] * (len(arguments) - scalars),
        out_specs=[SMEM] * len(outs) + [VMEM] * (len(passed) + 1 + len(sums)),
        scratch_shapes=scratch,
        compiler_params=params(20),
        cost_estimate=pl.CostEstimate(flops=1 << 20, bytes_accessed=1 << 10, transcendentals=0),
        name="moments",
    )(*arguments)


def solve_kernel(order_ref, *refs, kernels, planes):
    parts, out = refs[:-1], refs[-1]
    terms = len(TERMS)
    size = terms * planes
    lane = lax.broadcasted_iota(I32, (size, 128), 1)
    sub = lax.broadcasted_iota(I32, (size, 128), 0)

    def activity(index):
        plane, term = index % planes, index // planes
        order = jnp.zeros_like(index)
        for i in range(kernels):
            order = jnp.where(plane == i, order_ref[i], order)
        degree = jnp.zeros_like(index)
        for t, powers in enumerate(TERMS):
            degree = jnp.where(term == t, powers[0] + powers[1], degree)
        wanted = (plane == kernels) | ((plane < kernels) & (degree <= order))
        return jnp.where(wanted & (index < size), 1.0, 0.0)

    active_row = activity(lane[:8])
    active_row = jnp.concatenate([active_row] * (size // 8), axis=0)
    active_col = activity(sub)
    lane16 = lane[:planes]
    row8 = lax.broadcasted_iota(I32, (8, 128), 0)
    for q in range(out.shape[0]):
        moments = parts[0][q]
        for ref in parts[1:]:
            moments = moments + ref[q]
        rows = []
        for a in range(terms):
            row = jnp.zeros((planes, 128), F32)
            for b in range(terms):
                left, right = block_of(a, b)
                at = right % LEFT * planes
                place = right // LEFT * LEFT + left
                piece = moments[at : at + planes]
                if b != place:
                    piece = pltpu.roll(piece, ((b - place) * planes) % 128, 1)
                row = jnp.where(lane16 // planes == b, piece, row)
            rows.append(row)
        paired = jnp.concatenate(rows, axis=0)
        target = pltpu.roll(paired, size - (planes - 1), 1)
        masked = active_row * active_col * paired
        system = jnp.where(lane == sub, masked + (1.0 + RIDGE * masked), masked)
        system = jnp.where(lane == size, active_col * target, system)
        blocks = [system[8 * m : 8 * m + 8] for m in range(size // 8)]
        for at in range(size // 8):
            wanted = [i for i in range(8) if (8 * at + i) % planes <= kernels]
            columns = [
                {i: jnp.broadcast_to(block[:, 8 * at + i : 8 * at + i + 1], (8, 128)) for i in wanted}
                for block in blocks
            ]
            inner, here = columns[at], blocks[at]
            for i in wanted:
                pivot = jnp.broadcast_to(inner[i][i : i + 1], (8, 128))
                scale = pl.reciprocal(pivot, approx=True)
                scale = scale * (2.0 - pivot * scale)
                scale = scale * (2.0 - pivot * scale)
                line = jnp.broadcast_to(here[i : i + 1], (8, 128)) * scale
                here = jnp.where(row8 == i, line, here - inner[i] * line)
                for k in wanted:
                    if k > i:
                        entry = jnp.broadcast_to(inner[k][i : i + 1], (8, 128)) * scale
                        inner[k] = jnp.where(row8 == i, entry, inner[k] - inner[i] * entry)
            lines = {i: jnp.broadcast_to(here[i : i + 1], (8, 128)) for i in wanted}
            for m in range(size // 8):
                if m == at:
                    blocks[m] = here
                    continue
                terms_here = [columns[m][i] * lines[i] for i in wanted]
                while len(terms_here) > 1:
                    terms_here = [
                        functools.reduce(lambda a, b: a + b, terms_here[q : q + 2])
                        for q in range(0, len(terms_here), 2)
                    ]
                blocks[m] = blocks[m] - terms_here[0]
        answer = jnp.concatenate(blocks, axis=0)
        answer = jnp.broadcast_to(answer[:, size : size + 1], (size, 128))
        answer = jnp.where(sub % planes == lane % planes, answer, 0.0)
        lines = [
            jnp.sum(answer[t * planes : (t + 1) * planes], axis=0, keepdims=True)
            for t in range(terms)
        ]
        lines.append(jnp.zeros((8 - terms, 128), F32))
        out[q] = jnp.concatenate(lines, axis=0)


def solve(order, parts, kernels, planes):
    return pl.pallas_call(
        functools.partial(solve_kernel, kernels=kernels, planes=planes),
        out_shape=jax.ShapeDtypeStruct((parts[0].shape[0], 8, 128), F32),
        in_specs=[SMEM] + [VMEM] * len(parts),
        out_specs=VMEM,
        compiler_params=params(4),
        name="solve",
    )(order, *parts)


def difference_kernel(facts_ref, lists, *refs, sizes, tall):
    capacity, patches, ccds, share, tiles, kernels, planes = sizes
    coefs, stacks = refs[:ccds], refs[ccds : ccds + 2]
    out, table, split = refs[ccds + 2 :]
    strips, rows, columns = out.shape
    across = jnp.concatenate([across_rows(columns)] * (tall // 8), axis=0)
    across2 = across * across
    width = tall * planes
    lane = lax.broadcasted_iota(I32, (tall, width), 1)
    diagonal = lane // planes == lax.broadcasted_iota(I32, (tall, width), 0)
    is_science = diagonal & (lane % planes == planes - 1)
    sub = lax.broadcasted_iota(I32, (tall, columns), 0)

    def pieces(value):
        high = value.astype(BF16)
        rest = value - high.astype(F32)
        return high, rest.astype(BF16)

    for e in range(ccds):
        for k in range(share):
            d = place(facts_ref, patch_at(facts_ref, e, k, ccds, patches), patches)
            block = coefs[e][k]
            for t in range(len(TERMS)):
                line = jnp.concatenate([block[t : t + 1]] * (width // 128), axis=1)
                value = jnp.where(diagonal, -jnp.broadcast_to(line, (tall, width)), 0.0)
                table[d, t] = jnp.where(is_science, 1.0, value) if t == 0 else value
                if t == 2:
                    split[d, 0], split[d, 1] = pieces(value)

    for row, stack in zip((OWN, REST), stacks):
        count = lists[row, lists.shape[1] - 1]

        def step(t, carry, row=row, stack=stack, count=count):
            for i in range(FOUR):
                j = jnp.minimum(t * FOUR + i, count - 1)
                strip = lists[row, j]
                d = 0 if row == OWN else lists[GROUP, j]
                coef = [table[d, t] for t in range(len(TERMS))]
                twice = split[d, 0], split[d, 1]
                offset, good = facts_ref[ROW, strip], facts_ref[GOOD, strip]
                for h in range(rows // tall):
                    v = (2 * (offset + h * tall + sub) + 1).astype(F32) / PATCH_ROWS - 1.0
                    v = jnp.concatenate([v] * (width // 128), axis=1)
                    plain = coef[0] + v * (coef[3] + v * coef[1])
                    once = coef[4] + v * coef[5]
                    lhs = jnp.concatenate([*pieces(plain), *pieces(once), *twice], axis=0)
                    rhs = stack[j, h * width : (h + 1) * width, :]
                    got = jnp.dot(lhs, rhs, preferred_element_type=F32)
                    part = [got[x * tall : (x + 1) * tall] for x in range(6)]
                    value = (
                        (part[0] + part[1])
                        + across * (part[2] + part[3])
                        + across2 * (part[4] + part[5])
                    )
                    value = jnp.where(h * tall + sub < good, value, 0.0)
                    out[strip, h * tall : (h + 1) * tall, :] = value.astype(BF16)
            return carry

        lax.fori_loop(0, (count + FOUR - 1) // FOUR, step, 0)


def difference(facts, lists, coefs, stacks, shape, sizes):
    patches, planes, tall = sizes[1], sizes[-1], 16
    return pl.pallas_call(
        functools.partial(difference_kernel, sizes=sizes, tall=tall),
        out_shape=jax.ShapeDtypeStruct(shape, BF16),
        in_specs=[SMEM] * 2 + [VMEM] * (len(coefs) + len(stacks)),
        out_specs=VMEM,
        scratch_shapes=[
            pltpu.VMEM((patches, len(TERMS), tall, tall * planes), F32),
            pltpu.VMEM((patches, 2, tall, tall * planes), BF16),
        ],
        compiler_params=params(20),
        name="difference",
    )(facts, lists, *coefs, *stacks)


def shifted(value, axis, shift):
    size = lax.axis_size(axis)
    return lax.ppermute(value, axis, [(i, (i + shift) % size) for i in range(size)])


def body(
    science,
    strip_patch,
    strip_tile,
    strip_row,
    row_count,
    template,
    basis_rows,
    basis_cols,
    basis_order,
):
    patches, ccds = lax.axis_size("patch"), lax.axis_size("ccd")
    strips = science.shape[0]
    tiles = template.shape[0]
    kernels = basis_rows.shape[0]
    planes = -(-(kernels + 2) // 16) * 16
    capacity = max(2, 2 * strips // patches)
    share = -(-patches // ccds)
    sizes = (capacity, patches, ccds, share, tiles, kernels, planes)
    code = strip_patch * tiles + strip_tile
    me = lax.axis_index("patch")
    others = []
    for d in range(1, patches):
        owner = jnp.where(me + d >= patches, me + d - patches, me + d)
        others.append(shifted(code - owner * tiles, "patch", d))
    facts = jnp.stack(
        [code, strip_row, row_count, strip_patch]
        + [jnp.full_like(code, lax.axis_index(axis)) for axis in ("patch", "ccd")]
    )
    *tables, template = prepare(basis_rows, basis_cols, template, science.shape[1])
    chosen = select_tiles(others, template, capacity)
    plates = [shifted(tile, "patch", patches - d) for d, tile in enumerate(chosen, 1)]
    if patches > 8:
        plates = [jnp.concatenate(plates, axis=0)]
    lists, science, own_planes, before = moments_call(facts, None, science, tables, None, [template], sizes)
    planes_left, *scattered = moments_call(facts, lists, science, tables, before, plates, sizes)
    mine = scattered[0]
    for e in range(1, ccds):
        mine = mine + shifted(scattered[e], "ccd", e)
    parts = [mine] + [shifted(mine, "patch", d) for d in range(1, patches)]
    coefficients = solve(basis_order, parts, kernels, planes)
    coefs = [coefficients] + [shifted(coefficients, "ccd", ccds - e) for e in range(1, ccds)]
    return difference(facts, lists, coefs, [own_planes, planes_left], science.shape, sizes)


def solution(mesh):
    spread = P(("groups", "patch", "ccd"))
    return jax.shard_map(
        body,
        mesh=mesh,
        in_specs=(spread,) * 6 + (P(), P(), P()),
        out_specs=spread,
        check_vma=False,
    )
```
